32 devices in a mesh: row: 4 (over x, core), col: 8 (over z, y).
Axes of the slice: x: 2, y: 2, z: 4, core: 2. Of those that a mesh axis runs over, the one named last changes fastest.
Arguments:
- amplitudes: bfloat16 [8192, 4096], P('row', 'col'), may hold values from -6 to 6
- integrals: bfloat16 [4096, 2048], P('col'), may hold values from -0.125 to 0.125
- pair_index: int32 [8192], P('row'), may hold values from 0 to 39999, as said below
- partner: int32 [8192], P('row'), may hold values from 0 to 8191, as said below
- occ_energy: float32 [200], replicated, may hold values from -1 to -0.3
- vir_energy: float32 [2000], replicated, may hold values from 0.05 to 1
Outputs:
- increment: bfloat16 [8192, 4096], P('row', 'col')
The draws below stay inside these ranges and needn't reach their ends.
Inputs may be any that keep to these rules, and one draw needn't show every extreme that they name: `pair_index`: rows 0 and 1 hold the pairs (199, 199) and (0, 0); otherwise i and j are independent and uniform over 0 to 199. partner is an involution; partner[k] lies in row block (k // 2048) XOR (2), and pair_index[partner[k]] is pair_index[k] with i and j exchanged.
All inputs are finite; a program needn't handle non-finite values.
Results may differ from the reference program's by a relative error of at most 0.001.
Values may be sent and summed in bfloat16 or wider, within the bound.
No kernel may reach another device: no remote copies, remote signals or barrier semaphores. Data moves between devices by JAX's collectives and lax.ppermute only.
A program may use at most 128 MiB of HBM per device.

```python
import jax
import jax.numpy as jnp
from jax import lax

NOCC = 200
NV = 2000
STOPS = 4
IJ_DEV = 2048
BLK = 512
IJ = 8192
AB = 4096
N_COL = 8


def joint_pairs(key):
    base = jax.random.fold_in(key, 7)
    key_first, key_second, key_perm = jax.random.split(base, 3)
    half_rows = IJ // 2
    block_count = half_rows // IJ_DEV
    first = jax.random.randint(key_first, (half_rows,), 0, NOCC)
    second = jax.random.randint(key_second, (half_rows,), 0, NOCC)
    first = first.at[0].set(NOCC - 1).at[1].set(0)
    second = second.at[0].set(NOCC - 1).at[1].set(0)
    lower = first * NOCC + second
    upper_source = (second * NOCC + first).reshape(block_count, IJ_DEV)
    perm_keys = jax.random.split(key_perm, block_count)
    placed = jax.vmap(lambda k: jax.random.permutation(k, IJ_DEV))(perm_keys).astype(jnp.int32)
    inverse = jnp.argsort(placed, axis=1, stable=True).astype(jnp.int32)
    upper = jnp.take_along_axis(upper_source, inverse, axis=1).reshape(-1)
    block_start = (jnp.arange(block_count, dtype=jnp.int32) * IJ_DEV)[:, None]
    lower_partner = (half_rows + block_start + placed).reshape(-1)
    upper_partner = (block_start + inverse).reshape(-1)
    pair_values = jnp.concatenate([lower, upper]).astype(jnp.int32)
    partner_values = jnp.concatenate([lower_partner, upper_partner]).astype(jnp.int32)
    return (pair_values, partner_values)


def draw_pair_index(key, part):
    return joint_pairs(key)[0]


def draw_partner(key, part):
    return joint_pairs(key)[1]


def steps_of(key, extent, shards, least, top_value):
    def one(dim, blocks):
        steps = jax.random.uniform(jax.random.fold_in(jax.random.fold_in(key, 6), dim), (blocks,), jnp.float32, least / len(shards), top_value / len(shards))
        return jnp.repeat(jnp.exp(steps), extent[dim] // blocks).reshape((-1,) + (1,) * (len(extent) - dim - 1))

    gain = one(*shards[0])
    for cut in shards[1:]:
        gain = gain * one(*cut)
    return gain


def normal_values(own_key, dims, spread, most, cuts=(), kind=jnp.bfloat16):
    result = spread * jax.random.normal(own_key, dims, jnp.float32)
    if cuts:
        result = result * steps_of(own_key, dims, cuts, -0.22, 0.18)
    return jnp.clip(result, -most, most).astype(kind)


def setup_inputs(seed: int = 0) -> dict:
    key_list = jax.random.split(jax.random.key(seed), 7)
    amplitudes = normal_values(key_list[0], (IJ, AB), 1.0, 6.0, ((0, 4), (1, 8)))
    integrals = normal_values(key_list[1], (AB, STOPS * BLK), (STOPS * BLK) ** -0.5, 0.125, ((0, 8),))
    pair_index = draw_pair_index(jax.random.fold_in(key_list[6], 71), 0)
    partner = draw_partner(jax.random.fold_in(key_list[6], 71), 0)
    occ_energy = jnp.clip(jax.random.uniform(key_list[4], (NOCC,), jnp.float32, -1.0, -0.3), -1.0, -0.3)
    vir_energy = jnp.clip(jax.random.uniform(key_list[5], (NV,), jnp.float32, 0.05, 1.0), 0.05, 1.0)
    return {"amplitudes": amplitudes, "integrals": integrals, "pair_index": pair_index, "partner": partner, "occ_energy": occ_energy, "vir_energy": vir_energy}


def mirror_pairs(values):
    pair_width = values.shape[1]
    parity = (jnp.arange(pair_width, dtype=jnp.int32) % 2) == 0
    return jnp.where(parity[None, :], jnp.roll(values, -1, axis=1), jnp.roll(values, 1, axis=1))


def reference(amplitudes, integrals, pair_index, partner, occ_energy, vir_energy):
    ij_all = amplitudes.shape[0]
    pair_width = BLK
    occ_sum = occ_energy[pair_index // NOCC] + occ_energy[pair_index % NOCC]

    def one_block(block_index):
        running = jnp.zeros((ij_all, pair_width), jnp.float32)
        for stop_index in range(STOPS):
            source = ((block_index - stop_index) % N_COL).astype(jnp.int32)
            tile = lax.dynamic_slice_in_dim(amplitudes, source * pair_width, pair_width, 1)
            piece = lax.dynamic_slice(integrals, (source * pair_width, jnp.int32(stop_index * pair_width)), (pair_width, pair_width))
            running = running + jnp.dot(tile, piece, preferred_element_type=jnp.float32)
        opposite = mirror_pairs(jnp.take(running, partner, axis=0))
        global_pair = block_index * pair_width + jnp.arange(pair_width, dtype=jnp.int32)
        unordered = global_pair // 2
        vir_sum = vir_energy[unordered // NV] + vir_energy[unordered % NV]
        denom = vir_sum[None, :] - occ_sum[:, None]
        return ((running + opposite) / denom).astype(jnp.bfloat16)

    stacked = lax.map(one_block, jnp.arange(N_COL, dtype=jnp.int32))
    return jnp.transpose(stacked, (1, 0, 2)).reshape(ij_all, N_COL * pair_width)
```

```python
import functools

import jax
import jax.numpy as jnp
from jax import lax
from jax.experimental import pallas as pl
from jax.experimental.pallas import tpu as pltpu
from jax.sharding import PartitionSpec as P

NOCC = 200
NV = 2000
CHUNKS = 4
SCALE_ROWS = 16
TOP = 32767.0
STEPS = 64.0
TINY = 1e-33

VMEM = pl.BlockSpec(memory_space=pltpu.VMEM)
SMEM = pl.BlockSpec(memory_space=pltpu.SMEM)


def call(body, out_shape, flops, moved, scratch=()):
    def run(*operands):
        return pl.pallas_call(
            body,
            out_shape=out_shape,
            in_specs=[SMEM] + [VMEM] * (len(operands) - 1),
            out_specs=jax.tree.map(lambda _: VMEM, out_shape),
            scratch_shapes=list(scratch),
            compiler_params=pltpu.CompilerParams(vmem_limit_bytes=48 * 1024 * 1024),
            cost_estimate=pl.CostEstimate(flops=flops, bytes_accessed=moved, transcendentals=0),
        )(*operands)

    return run


def swap_matrix(width):
    down = lax.broadcasted_iota(jnp.int32, (width, width), 0)
    across = lax.broadcasted_iota(jnp.int32, (width, width), 1)
    return jnp.where(down == (across ^ 1), 1.0, 0.0).astype(jnp.bfloat16)


def mirrored(values, swap):
    return jnp.dot(values, swap, preferred_element_type=jnp.float32).astype(jnp.bfloat16)


def mirror_kernel(flags, integrals, out):
    width = integrals.shape[0]
    swap = swap_matrix(width)
    for stop in range(integrals.shape[1] // width):
        cols = pl.ds(stop * width, width)
        out[:, cols] = mirrored(integrals[:, cols], swap)


def align_kernel(index, send, flags, slots, amplitudes, out):
    rows = amplitudes.shape[0]
    chunk = out.shape[0]
    upper = flags[0]
    side = 1 - upper if send else upper
    first = side * (rows // 2) + index * chunk

    @pl.when(upper == 0)
    def _():
        out[...] = amplitudes[pl.ds(pl.multiple_of(first, chunk), chunk), :]

    @pl.when(upper == 1)
    def _():
        wanted = first + lax.broadcasted_iota(jnp.int32, (chunk, rows), 0)
        pick = jnp.where(slots[...] == wanted, 1.0, 0.0).astype(jnp.bfloat16)
        out[...] = jnp.dot(pick, amplitudes[...], preferred_element_type=jnp.float32).astype(jnp.bfloat16)


def product(own, other, direct, swapped):
    return jnp.dot(own[...], direct[...], preferred_element_type=jnp.float32) + jnp.dot(
        other[...], swapped[...], preferred_element_type=jnp.float32
    )


def code(values, out):
    rows = values.shape[0]
    top = jnp.max(jnp.abs(values), axis=0, keepdims=True)
    level = jnp.ceil(STEPS * jnp.log2(jnp.maximum(top, TINY) * (1.0001 / TOP)))
    coded = jnp.round(values * jnp.exp2(level * (-1.0 / STEPS)))
    out[pl.ds(0, rows), :] = coded.astype(jnp.int32).astype(jnp.int16)
    spread = jnp.broadcast_to(level.astype(jnp.int32), (SCALE_ROWS, values.shape[1]))
    out[pl.ds(rows, SCALE_ROWS), :] = spread.astype(jnp.int16)


def decode(coded):
    rows = coded.shape[0] - SCALE_ROWS
    level = coded[pl.ds(rows, SCALE_ROWS), :].astype(jnp.int32).astype(jnp.float32)[0:1, :]
    return coded[pl.ds(0, rows), :].astype(jnp.int32).astype(jnp.float32) * jnp.exp2(level * (1.0 / STEPS))


def first_kernel(flags, own, other, direct, swapped, out):
    code(product(own, other, direct, swapped), out)


def second_kernel(flags, own, other, direct, swapped, arrived, out):
    code(product(own, other, direct, swapped) + decode(arrived), out)


def third_kernel(flags, own, other, direct, swapped, arrived, out):
    here = jnp.where(flags[1] == 0, 1.0, 0.0)
    code(product(own, other, direct, swapped) + decode(arrived) * here, out)


def last_kernel(flags, own, other, direct, swapped, crossed, arrived, occ_sum, vir_sum, out):
    here = jnp.where(flags[1] == 1, 1.0, 0.0)
    total = product(own, other, direct, swapped) + decode(arrived) + decode(crossed) * here
    out[...] = (total / (vir_sum[...] - occ_sum[...])).astype(jnp.bfloat16)


def place_kernel(count, flags, slots, *refs):
    own, other, out, whole = refs[:count], refs[count : 2 * count], refs[-2], refs[-1]
    upper = flags[0]
    rows, width = out.shape
    chunk = rows // (2 * count)
    swap = swap_matrix(width)
    for index in range(count):
        here = upper * (rows // 2) + index * chunk
        there = (1 - upper) * (rows // 2) + index * chunk
        whole[pl.ds(pl.multiple_of(here, chunk), chunk), :] = own[index][...]
        whole[pl.ds(pl.multiple_of(there, chunk), chunk), :] = mirrored(other[index][...], swap)

    @pl.when(upper == 0)
    def _():
        out[...] = whole[...]

    @pl.when(upper == 1)
    def _():
        block = 256

        @pl.loop(0, rows // block)
        def _(step):
            part = pl.ds(pl.multiple_of(step * block, block), block)
            source = lax.broadcasted_iota(jnp.int32, (block, rows), 1)
            pick = jnp.where(slots[part, :] == source, 1.0, 0.0).astype(jnp.bfloat16)
            out[part, :] = jnp.dot(pick, whole[...], preferred_element_type=jnp.float32).astype(jnp.bfloat16)


def table_lookup(table, positions):
    slots = jnp.arange(table.shape[0], dtype=jnp.int32)
    return jnp.sum(jnp.where(positions[:, None] == slots[None, :], table[None, :], 0.0), axis=1)


def across_rows(value):
    count = lax.axis_size("row")
    return lax.ppermute(value, "row", [(i, i ^ (count // 2)) for i in range(count)])


def across_pair(value):
    return lax.ppermute(value, "col", [(i, i ^ 1) for i in range(lax.axis_size("col"))])


def two_along(value):
    count = lax.axis_size("col")
    return lax.ppermute(value, "col", [(i, (i + 2) % count) for i in range(count)])


def shards(amplitudes, integrals, pair_index, partner, occ_energy, vir_energy):
    rows, width = amplitudes.shape
    chunk = rows // (2 * CHUNKS)
    upper = (lax.axis_index("row") // (lax.axis_size("row") // 2)).astype(jnp.int32)
    odd = (lax.axis_index("col") % 2).astype(jnp.int32)
    flags = jnp.stack([upper, odd])
    slots = partner % rows

    chunk_shape = jax.ShapeDtypeStruct((chunk, width), jnp.bfloat16)
    coded_shape = jax.ShapeDtypeStruct((chunk + SCALE_ROWS, width), jnp.int16)
    pair_bytes = 4 * chunk * width + 4 * width * width

    def align(index, send):
        return call(
            functools.partial(align_kernel, index, send), chunk_shape, 2 * chunk * rows * width, 2 * rows * width
        )(flags, slots[None, :], amplitudes)

    def stage(body, out_shape, *operands):
        return call(body, out_shape, 4 * chunk * width * width, pair_bytes + 2 * chunk * width)(flags, *operands)

    sent = [align(index, True) for index in range(CHUNKS)]
    other = [across_rows(value) for value in sent]
    own = [align(index, False) for index in range(CHUNKS)]

    swapped = call(
        mirror_kernel, jax.ShapeDtypeStruct(integrals.shape, jnp.bfloat16), 8 * width**3, 4 * integrals.size
    )(flags, integrals)
    direct = [integrals[:, s * width : (s + 1) * width] for s in range(4)]
    swapped = [swapped[:, s * width : (s + 1) * width] for s in range(4)]

    occ_sum = table_lookup(occ_energy, pair_index // NOCC) + table_lookup(occ_energy, pair_index % NOCC)
    occ_upper = across_rows(occ_sum[rows // 2 :])
    occ_sum = jnp.where(upper == 0, occ_sum[: rows // 2], occ_upper)[:, None]
    global_pair = lax.axis_index("col") * width + jnp.arange(width, dtype=jnp.int32)
    unordered = global_pair // 2
    vir_sum = table_lookup(vir_energy, unordered // NV) + table_lookup(vir_energy, unordered % NV)
    vir_sum = vir_sum[None, :]

    done = []
    for index in range(CHUNKS):
        pair = (own[index], other[index])
        moved = two_along(stage(first_kernel, coded_shape, *pair, direct[3], swapped[3]))
        crossed = across_pair(stage(second_kernel, coded_shape, *pair, direct[1], swapped[1], moved))
        arrived = two_along(stage(third_kernel, coded_shape, *pair, direct[2], swapped[2], crossed))
        done.append(
            stage(
                last_kernel,
                chunk_shape,
                *pair,
                direct[0],
                swapped[0],
                crossed,
                arrived,
                occ_sum[index * chunk : (index + 1) * chunk],
                vir_sum,
            )
        )
    theirs = [across_rows(value) for value in done]
    return call(
        functools.partial(place_kernel, CHUNKS),
        jax.ShapeDtypeStruct((rows, width), jnp.bfloat16),
        2 * rows * rows * width,
        4 * rows * width,
        [pltpu.VMEM((rows, width), jnp.bfloat16)],
    )(flags, slots[:, None], *done, *theirs)


def solution(mesh):
    in_specs = (P("row", "col"), P("col", None), P("row"), P("row"), P(), P())
    out_specs = P("row", "col")
    return jax.shard_map(shards, mesh=mesh, in_specs=in_specs, out_specs=out_specs, check_vma=False)
```

```python
import functools

import jax
import jax.numpy as jnp
from jax import lax
from jax.experimental import pallas as pl
from jax.experimental.pallas import tpu as pltpu
from jax.sharding import PartitionSpec as P

NOCC = 200
NV = 2000
CHUNKS = 4
SCALE_ROWS = 16
TOP = 32767.0
STEPS = 64.0
TINY = 1e-33
VMEM_LIMIT = 16 * 1024 * 1024

VMEM = pl.BlockSpec(memory_space=pltpu.VMEM)
SMEM = pl.BlockSpec(memory_space=pltpu.SMEM)
ANY = pl.BlockSpec(memory_space=pl.ANY)


def call(body, out_shape, flops, moved, operands, after=()):
    count = len(operands)

    def kernel(*refs):
        body(*refs[:count], *refs[count + len(after) :])

    return pl.pallas_call(
        kernel,
        out_shape=out_shape,
        in_specs=[SMEM] + [VMEM] * (count - 1) + [ANY] * len(after),
        out_specs=jax.tree.map(lambda _: VMEM, out_shape),
        compiler_params=pltpu.CompilerParams(vmem_limit_bytes=VMEM_LIMIT),
        cost_estimate=pl.CostEstimate(flops=flops, bytes_accessed=moved, transcendentals=0),
    )(*operands, *after)


def swap_matrix(width):
    down = lax.broadcasted_iota(jnp.int32, (width, width), 0)
    across = lax.broadcasted_iota(jnp.int32, (width, width), 1)
    return jnp.where(down == (across ^ 1), 1.0, 0.0).astype(jnp.bfloat16)


def exact_dot(left, right):
    return jnp.dot(left, right, preferred_element_type=jnp.float32).astype(jnp.bfloat16)


def mirror_kernel(flags, integrals, out):
    width = integrals.shape[0]
    swap = swap_matrix(width)
    for stop in range(integrals.shape[1] // width):
        cols = pl.ds(stop * width, width)
        out[:, cols] = exact_dot(integrals[:, cols], swap)


def align_kernel(begin, send, flags, partner, amplitudes, *outs):
    rows = amplitudes.shape[0]
    chunk = outs[0].shape[0]
    upper = flags[0]
    side = 1 - upper if send else upper
    first = side * (rows // 2) + begin

    @pl.when(upper == 0)
    def _():
        for index, out in enumerate(outs):
            out[...] = amplitudes[pl.ds(pl.multiple_of(first + index * chunk, chunk), chunk), :]

    @pl.when(upper == 1)
    def _():
        for index, out in enumerate(outs):
            wanted = flags[2] + first + index * chunk + lax.broadcasted_iota(jnp.int32, (chunk, rows), 0)
            pick = jnp.where(partner[...] == wanted, 1.0, 0.0).astype(jnp.bfloat16)
            out[...] = exact_dot(pick, amplitudes[...])


def product(stop, own, other, integrals, mirrored):
    cols = pl.ds(stop * own.shape[1], own.shape[1])
    return jnp.dot(own[...], integrals[:, cols], preferred_element_type=jnp.float32) + jnp.dot(
        other[...], mirrored[:, cols], preferred_element_type=jnp.float32
    )


def code(values, out):
    rows = values.shape[0]
    top = jnp.max(jnp.abs(values), axis=0, keepdims=True)
    level = jnp.ceil(STEPS * jnp.log2(jnp.maximum(top, TINY) * (1.0001 / TOP)))
    coded = jnp.round(values * jnp.exp2(level * (-1.0 / STEPS)))
    out[pl.ds(0, rows), :] = coded.astype(jnp.int32).astype(jnp.int16)
    spread = jnp.broadcast_to(level.astype(jnp.int32), (SCALE_ROWS, values.shape[1]))
    out[pl.ds(rows, SCALE_ROWS), :] = spread.astype(jnp.int16)


def decode(coded):
    rows = coded.shape[0] - SCALE_ROWS
    level = coded[pl.ds(rows, SCALE_ROWS), :].astype(jnp.int32).astype(jnp.float32)[0:1, :]
    return coded[pl.ds(0, rows), :].astype(jnp.int32).astype(jnp.float32) * jnp.exp2(level * (1.0 / STEPS))


def first_kernel(flags, own, other, integrals, mirrored, out):
    code(product(3, own, other, integrals, mirrored), out)


def second_kernel(flags, own, other, integrals, mirrored, arrived, out):
    code(product(1, own, other, integrals, mirrored) + decode(arrived), out)


def third_kernel(flags, own, other, integrals, mirrored, crossed, out):
    here = jnp.where(flags[1] == 0, 1.0, 0.0)
    code(product(2, own, other, integrals, mirrored) + decode(crossed) * here, out)


def last_kernel(index, flags, own, other, integrals, mirrored, crossed, arrived, occ_sum, vir_sum, out):
    chunk, width = out.shape
    here = jnp.where(flags[1] == 1, 1.0, 0.0)
    total = product(0, own, other, integrals, mirrored) + decode(arrived) + decode(crossed) * here
    occ_rows = occ_sum[:, pl.ds(index * chunk, chunk)]
    occ_down = jnp.broadcast_to(occ_rows, (128, chunk)).T
    for lane in range(0, width, 128):
        denom = vir_sum[:, lane : lane + 128] - occ_down
        out[:, lane : lane + 128] = (total[:, lane : lane + 128] / denom).astype(jnp.bfloat16)


def place_kernel(index, flags, partner, own, other, *refs):
    out = refs[-1]
    rows, width = out.shape
    chunk = own.shape[0]
    upper = flags[0]
    here = upper * (rows // 2) + index * chunk
    there = (1 - upper) * (rows // 2) + index * chunk
    opposite = exact_dot(other[...], swap_matrix(width))

    @pl.when(upper == 0)
    def _():
        if index:
            out[...] = refs[0][...]
        out[pl.ds(pl.multiple_of(here, chunk), chunk), :] = own[...]
        out[pl.ds(pl.multiple_of(there, chunk), chunk), :] = opposite

    @pl.when(upper == 1)
    def _():
        block = 256
        lanes = lax.broadcasted_iota(jnp.int32, (block, chunk), 1) + flags[2]
        for begin in range(0, rows, block):
            part = pl.ds(begin, block)
            slots = partner[part, :]
            pick_here = jnp.where(slots == lanes + here, 1.0, 0.0).astype(jnp.bfloat16)
            pick_there = jnp.where(slots == lanes + there, 1.0, 0.0).astype(jnp.bfloat16)
            found = jnp.dot(pick_here, own[...], preferred_element_type=jnp.float32)
            found += jnp.dot(pick_there, opposite, preferred_element_type=jnp.float32)
            if index:
                found += refs[0][part, :].astype(jnp.float32)
            out[part, :] = found.astype(jnp.bfloat16)


def table_lookup(table, positions):
    slots = jnp.arange(table.shape[0], dtype=jnp.int32)
    return jnp.sum(jnp.where(positions[:, None] == slots[None, :], table[None, :], 0.0), axis=1)


def across_rows(value):
    count = lax.axis_size("row")
    return lax.ppermute(value, "row", [(i, i ^ (count // 2)) for i in range(count)])


def across_pair(value):
    return lax.ppermute(value, "col", [(i, i ^ 1) for i in range(lax.axis_size("col"))])


def two_along(value):
    count = lax.axis_size("col")
    return lax.ppermute(value, "col", [(i, (i + 2) % count) for i in range(count)])


def shards(amplitudes, integrals, pair_index, partner, occ_energy, vir_energy):
    rows, width = amplitudes.shape
    half = rows // 2
    chunk = half // CHUNKS
    row_count = lax.axis_size("row")
    row = lax.axis_index("row")
    upper = (row // (row_count // 2)).astype(jnp.int32)
    odd = (lax.axis_index("col") % 2).astype(jnp.int32)
    partner_base = ((row ^ (row_count // 2)) * rows).astype(jnp.int32)
    flags = jnp.stack([upper, odd, partner_base])

    chunk_shape = jax.ShapeDtypeStruct((chunk, width), jnp.bfloat16)
    coded_shape = jax.ShapeDtypeStruct((chunk + SCALE_ROWS, width), jnp.int16)
    whole_shape = jax.ShapeDtypeStruct((rows, width), jnp.bfloat16)

    def align(begin, count, send, after=()):
        return call(
            functools.partial(align_kernel, begin * chunk, send),
            [chunk_shape] * count,
            2 * count * chunk * rows * width,
            2 * rows * width,
            (flags, partner[None, :], amplitudes),
            after,
        )

    def stage(body, out_shape, *operands):
        return call(body, out_shape, 4 * chunk * width * width, 16 * chunk * width, (flags, *operands))

    sent = align(0, 1, True)
    mirrored = call(
        mirror_kernel,
        jax.ShapeDtypeStruct(integrals.shape, jnp.bfloat16),
        8 * width**3,
        4 * integrals.size,
        (flags, integrals),
        (sent[0],),
    )
    sent += align(1, 1, True, (mirrored,))
    own = align(0, CHUNKS, False, (sent[1],))
    sent += align(2, CHUNKS - 2, True, (own[0],))
    other = [across_rows(value) for value in sent]

    occ_sum = table_lookup(occ_energy, pair_index // NOCC) + table_lookup(occ_energy, pair_index % NOCC)
    occ_sum = jnp.where(upper == 0, occ_sum[:half], across_rows(occ_sum[half:]))[None, :]
    global_pair = lax.axis_index("col") * width + jnp.arange(width, dtype=jnp.int32)
    unordered = global_pair // 2
    vir_sum = table_lookup(vir_energy, unordered // NV) + table_lookup(vir_energy, unordered % NV)
    vir_sum = vir_sum[None, :]

    placed = ()
    for index in range(CHUNKS):
        inputs = (own[index], other[index], integrals, mirrored)
        moved = two_along(stage(first_kernel, coded_shape, *inputs))
        crossed = across_pair(stage(second_kernel, coded_shape, *inputs, moved))
        arrived = two_along(stage(third_kernel, coded_shape, *inputs, crossed))
        done = stage(
            functools.partial(last_kernel, index), chunk_shape, *inputs, crossed, arrived, occ_sum, vir_sum
        )
        placed = (
            call(
                functools.partial(place_kernel, index),
                whole_shape,
                4 * chunk * rows * width,
                4 * rows * width,
                (flags, partner[:, None], done, across_rows(done), *placed),
            ),
        )
    return placed[0]


def solution(mesh):
    in_specs = (P("row", "col"), P("col", None), P("row"), P("row"), P(), P())
    out_specs = P("row", "col")
    return jax.shard_map(shards, mesh=mesh, in_specs=in_specs, out_specs=out_specs, check_vma=False)
```

```python
import functools

import jax
import jax.numpy as jnp
from jax import lax
from jax.experimental import pallas as pl
from jax.experimental.pallas import tpu as pltpu
from jax.sharding import PartitionSpec as P

NOCC = 200
NV = 2000
CHUNKS = 4
SCALE_ROWS = 16
TOP = 32767.0
STEPS = 64.0
TINY = 1e-33
VMEM_LIMIT = 8 * 1024 * 1024
ORDER = (
    ((1, 0), (1, 1), (2, 0), (1, 2), (2, 1), (1, 3), (3, 0), (2, 2), (3, 1), (2, 3))
    + ((3, 2), (4, 0), (3, 3), (4, 1), (5, 0), (4, 2), (5, 1), (4, 3), (5, 2), (5, 3))
)

VMEM = pl.BlockSpec(memory_space=pltpu.VMEM)
SMEM = pl.BlockSpec(memory_space=pltpu.SMEM)
ANY = pl.BlockSpec(memory_space=pl.ANY)


def call(body, out_shape, operands, after=()):
    count = len(operands)

    def kernel(*refs):
        body(*refs[:count], *refs[count + len(after) :])

    return pl.pallas_call(
        kernel,
        out_shape=out_shape,
        in_specs=[SMEM] + [VMEM] * (count - 1) + [ANY] * len(after),
        out_specs=jax.tree.map(lambda _: VMEM, out_shape),
        compiler_params=pltpu.CompilerParams(vmem_limit_bytes=VMEM_LIMIT),
        cost_estimate=pl.CostEstimate(flops=1, bytes_accessed=1, transcendentals=0),
    )(*operands, *after)


def swap_matrix(width):
    down = lax.broadcasted_iota(jnp.int32, (width, width), 0)
    across = lax.broadcasted_iota(jnp.int32, (width, width), 1)
    return jnp.where(down == (across ^ 1), 1.0, 0.0).astype(jnp.bfloat16)


def exact_dot(left, right):
    return jnp.dot(left, right, preferred_element_type=jnp.float32).astype(jnp.bfloat16)


def mirror_kernel(flags, integrals, *outs):
    width = integrals.shape[0]
    swap = swap_matrix(width)
    for stop, out in enumerate(outs):
        block = integrals[:, pl.ds(stop * width, width)]
        out[pl.ds(0, width), :] = block
        out[pl.ds(width, width), :] = exact_dot(block, swap)


def align_kernel(begin, send, flags, partner, amplitudes, *outs):
    rows = amplitudes.shape[0]
    chunk = outs[0].shape[0]
    upper = flags[0]
    side = 1 - upper if send else upper
    first = side * (rows // 2) + begin

    @pl.when(upper == 0)
    def _():
        for index, out in enumerate(outs):
            out[...] = amplitudes[pl.ds(pl.multiple_of(first + index * chunk, chunk), chunk), :]

    @pl.when(upper == 1)
    def _():
        for index, out in enumerate(outs):
            wanted = flags[2] + first + index * chunk + lax.broadcasted_iota(jnp.int32, (chunk, rows), 0)
            pick = jnp.where(partner[...] == wanted, 1.0, 0.0).astype(jnp.bfloat16)
            out[...] = exact_dot(pick, amplitudes[...])


def product(own, other, factor):
    width = own.shape[1]
    return jnp.dot(own[...], factor[pl.ds(0, width), :], preferred_element_type=jnp.float32) + jnp.dot(
        other[...], factor[pl.ds(width, width), :], preferred_element_type=jnp.float32
    )


def code(values, out):
    rows = values.shape[0]
    top = jnp.max(jnp.abs(values), axis=0, keepdims=True)
    level = jnp.ceil(STEPS * jnp.log2(jnp.maximum(top, TINY) * (1.0001 / TOP)))
    coded = jnp.round(values * jnp.exp2(level * (-1.0 / STEPS)))
    out[pl.ds(0, rows), :] = coded.astype(jnp.int32).astype(jnp.int16)
    spread = jnp.broadcast_to(level.astype(jnp.int32), (SCALE_ROWS, values.shape[1]))
    out[pl.ds(rows, SCALE_ROWS), :] = spread.astype(jnp.int16)


def decode(coded):
    rows = coded.shape[0] - SCALE_ROWS
    level = coded[pl.ds(rows, SCALE_ROWS), :].astype(jnp.int32).astype(jnp.float32)[0:1, :]
    return coded[pl.ds(0, rows), :].astype(jnp.int32).astype(jnp.float32) * jnp.exp2(level * (1.0 / STEPS))


def first_kernel(flags, own, other, factor, out):
    code(product(own, other, factor), out)


def second_kernel(flags, own, other, factor, arrived, out):
    code(product(own, other, factor) + decode(arrived), out)


def third_kernel(flags, own, other, factor, crossed, out):
    here = jnp.where(flags[1] == 0, 1.0, 0.0)
    code(product(own, other, factor) + decode(crossed) * here, out)


def last_kernel(index, flags, own, other, factor, crossed, arrived, occ_sum, vir_sum, out):
    chunk, width = out.shape
    here = jnp.where(flags[1] == 1, 1.0, 0.0)
    total = product(own, other, factor) + decode(arrived) + decode(crossed) * here
    occ_rows = occ_sum[:, pl.ds(index * chunk, chunk)]
    occ_down = jnp.broadcast_to(occ_rows, (128, chunk)).T
    for lane in range(0, width, 128):
        denom = vir_sum[:, lane : lane + 128] - occ_down
        out[:, lane : lane + 128] = (total[:, lane : lane + 128] / denom).astype(jnp.bfloat16)


def place_kernel(index, flags, partner, own, other, *refs):
    out = refs[-1]
    rows, width = out.shape
    chunk = own.shape[0]
    upper = flags[0]
    here = upper * (rows // 2) + index * chunk
    there = (1 - upper) * (rows // 2) + index * chunk
    opposite = exact_dot(other[...], swap_matrix(width))

    @pl.when(upper == 0)
    def _():
        if index:
            out[...] = refs[0][...]
        out[pl.ds(pl.multiple_of(here, chunk), chunk), :] = own[...]
        out[pl.ds(pl.multiple_of(there, chunk), chunk), :] = opposite

    @pl.when(upper == 1)
    def _():
        block = 256
        lanes = lax.broadcasted_iota(jnp.int32, (block, chunk), 1) + flags[2]
        for begin in range(0, rows, block):
            part = pl.ds(begin, block)
            slots = partner[part, :]
            pick_here = jnp.where(slots == lanes + here, 1.0, 0.0).astype(jnp.bfloat16)
            pick_there = jnp.where(slots == lanes + there, 1.0, 0.0).astype(jnp.bfloat16)
            found = jnp.dot(pick_here, own[...], preferred_element_type=jnp.float32)
            found += jnp.dot(pick_there, opposite, preferred_element_type=jnp.float32)
            if index:
                found += refs[0][part, :].astype(jnp.float32)
            out[part, :] = found.astype(jnp.bfloat16)


def table_lookup(table, positions):
    slots = jnp.arange(table.shape[0], dtype=jnp.int32)
    return jnp.sum(jnp.where(positions[:, None] == slots[None, :], table[None, :], 0.0), axis=1)


def across_rows(value):
    count = lax.axis_size("row")
    return lax.ppermute(value, "row", [(i, i ^ (count // 2)) for i in range(count)])


def across_pair(value):
    return lax.ppermute(value, "col", [(i, i ^ 1) for i in range(lax.axis_size("col"))])


def two_along(value):
    count = lax.axis_size("col")
    return lax.ppermute(value, "col", [(i, (i + 2) % count) for i in range(count)])


def shards(amplitudes, integrals, pair_index, partner, occ_energy, vir_energy):
    rows, width = amplitudes.shape
    half = rows // 2
    chunk = half // CHUNKS
    row_count = lax.axis_size("row")
    row = lax.axis_index("row")
    upper = (row // (row_count // 2)).astype(jnp.int32)
    odd = (lax.axis_index("col") % 2).astype(jnp.int32)
    partner_base = ((row ^ (row_count // 2)) * rows).astype(jnp.int32)
    flags = jnp.stack([upper, odd, partner_base])

    chunk_shape = jax.ShapeDtypeStruct((chunk, width), jnp.bfloat16)
    coded_shape = jax.ShapeDtypeStruct((chunk + SCALE_ROWS, width), jnp.int16)
    whole_shape = jax.ShapeDtypeStruct((rows, width), jnp.bfloat16)

    def align(begin, count, send, after=()):
        return call(
            functools.partial(align_kernel, begin * chunk, send),
            [chunk_shape] * count,
            (flags, partner[None, :], amplitudes),
            after,
        )

    sent = align(0, 1, True)
    factors = call(
        mirror_kernel, [jax.ShapeDtypeStruct((2 * width, width), jnp.bfloat16)] * 4, (flags, integrals), sent[:1]
    )
    sent += align(1, 1, True, factors[:1])
    own = align(0, CHUNKS, False, sent[1:2])
    sent += align(2, CHUNKS - 2, True, own[:1])
    other = [across_rows(value) for value in sent]

    occ_sum = table_lookup(occ_energy, pair_index // NOCC) + table_lookup(occ_energy, pair_index % NOCC)
    occ_sum = jnp.where(upper == 0, occ_sum[:half], across_rows(occ_sum[half:]))[None, :]
    global_pair = lax.axis_index("col") * width + jnp.arange(width, dtype=jnp.int32)
    unordered = global_pair // 2
    vir_sum = table_lookup(vir_energy, unordered // NV) + table_lookup(vir_energy, unordered % NV)
    vir_sum = vir_sum[None, :]

    moved, crossed, arrived, done, placed = {}, {}, {}, {}, ()
    last = sent[CHUNKS - 1]
    for step, index in ORDER:
        pair = (flags, own[index], other[index])
        if step == 1:
            last = call(first_kernel, coded_shape, (*pair, factors[3]), (last,))
            moved[index] = two_along(last)
        elif step == 2:
            last = call(second_kernel, coded_shape, (*pair, factors[1], moved[index]), (last,))
            crossed[index] = across_pair(last)
        elif step == 3:
            last = call(third_kernel, coded_shape, (*pair, factors[2], crossed[index]), (last,))
            arrived[index] = two_along(last)
        elif step == 4:
            last = call(
                functools.partial(last_kernel, index),
                chunk_shape,
                (*pair, factors[0], crossed[index], arrived[index], occ_sum, vir_sum),
                (last,),
            )
            done[index] = (last, across_rows(last))
        else:
            last = call(
                functools.partial(place_kernel, index),
                whole_shape,
                (flags, partner[:, None], *done[index], *placed),
                (last,),
            )
            placed = (last,)
    return last


def solution(mesh):
    in_specs = (P("row", "col"), P("col", None), P("row"), P("row"), P(), P())
    out_specs = P("row", "col")
    return jax.shard_map(shards, mesh=mesh, in_specs=in_specs, out_specs=out_specs, check_vma=False)
```

```python
import functools

import jax
import jax.numpy as jnp
from jax import lax
from jax.experimental import pallas as pl
from jax.experimental.pallas import tpu as pltpu
from jax.sharding import PartitionSpec as P

NOCC = 200
NV = 2000
CHUNKS = 4
SCALE_ROWS = 16
TOP = 32767.0
STEPS = 64.0
TINY = 1e-33
LANES = 128
VMEM_LIMIT = 8 * 1024 * 1024
KERNEL_BYTES = 300 * 1024
ORDER = (
    (("align", 0), ("align", 1), ("energy", 0), ("first", 0), ("align", 2), ("first", 1))
    + (("align", 3), ("first", 2), ("second", 0), ("second", 1), ("first", 3), ("third", 0))
    + (("second", 2), ("third", 1), ("second", 3), ("third", 2), ("last", 0), ("third", 3))
    + (("last", 1), ("last", 2), ("place", 0), ("last", 3), ("place", 1), ("place", 2))
    + (("place", 3),)
)
ALIGNED = (
    ((0, True),),
    ((1, True), (0, False)),
    ((2, True), (1, False)),
    ((3, True), (2, False), (3, False)),
)

VMEM = pl.BlockSpec(memory_space=pltpu.VMEM)
SMEM = pl.BlockSpec(memory_space=pltpu.SMEM)
ANY = pl.BlockSpec(memory_space=pl.ANY)


def call(body, out_shape, operands, after=()):
    count = len(operands)

    def kernel(*refs):
        body(*refs[:count], *refs[count + len(after) :])

    return pl.pallas_call(
        kernel,
        out_shape=out_shape,
        in_specs=[SMEM] + [VMEM] * (count - 1) + [ANY] * len(after),
        out_specs=jax.tree.map(lambda _: VMEM, out_shape),
        compiler_params=pltpu.CompilerParams(vmem_limit_bytes=VMEM_LIMIT),
        cost_estimate=pl.CostEstimate(flops=1, bytes_accessed=KERNEL_BYTES, transcendentals=0),
    )(*operands, *after)


def exchanged(values):
    even = lax.broadcasted_iota(jnp.int32, (values.shape[0], LANES), 1) % 2 == 0
    parts = []
    for lane in range(0, values.shape[1], LANES):
        part = values[:, lane : lane + LANES]
        parts.append(jnp.where(even, pltpu.roll(part, LANES - 1, 1), pltpu.roll(part, 1, 1)))
    return jnp.concatenate(parts, axis=1)


def align_kernel(wanted, flags, partner, amplitudes, *outs):
    rows = amplitudes.shape[0]
    chunk = outs[0].shape[0]
    upper = flags[0]

    def first(index):
        begin, send = wanted[index]
        return (1 - upper if send else upper) * (rows // 2) + begin

    @pl.when(upper == 0)
    def _():
        for index, out in enumerate(outs):
            out[...] = amplitudes[pl.ds(pl.multiple_of(first(index), chunk), chunk), :]

    @pl.when(upper == 1)
    def _():
        for index, out in enumerate(outs):
            target = flags[2] + first(index) + lax.broadcasted_iota(jnp.int32, (chunk, rows), 0)
            pick = jnp.where(partner[...] == target, 1.0, 0.0).astype(jnp.bfloat16)
            out[...] = jnp.dot(pick, amplitudes[...], preferred_element_type=jnp.float32).astype(jnp.bfloat16)


def product(stop, own, other, integrals):
    factor = integrals[:, pl.ds(stop * own.shape[1], own.shape[1])]
    direct = jnp.dot(own[...], factor, preferred_element_type=jnp.float32)
    return direct + exchanged(jnp.dot(other[...], factor, preferred_element_type=jnp.float32))


def code(values, out):
    rows = values.shape[0]
    top = jnp.max(jnp.abs(values), axis=0, keepdims=True)
    level = jnp.ceil(STEPS * jnp.log2(jnp.maximum(top, TINY) * (1.0001 / TOP)))
    coded = jnp.round(values * jnp.exp2(level * (-1.0 / STEPS)))
    out[pl.ds(0, rows), :] = coded.astype(jnp.int32).astype(jnp.int16)
    spread = jnp.broadcast_to(level.astype(jnp.int32), (SCALE_ROWS, values.shape[1]))
    out[pl.ds(rows, SCALE_ROWS), :] = spread.astype(jnp.int16)


def decode(coded):
    rows = coded.shape[0] - SCALE_ROWS
    level = coded[pl.ds(rows, SCALE_ROWS), :].astype(jnp.int32).astype(jnp.float32)[0:1, :]
    return coded[pl.ds(0, rows), :].astype(jnp.int32).astype(jnp.float32) * jnp.exp2(level * (1.0 / STEPS))


def first_kernel(flags, own, other, integrals, out):
    code(product(3, own, other, integrals), out)


def second_kernel(flags, own, other, integrals, arrived, out):
    code(product(1, own, other, integrals) + decode(arrived), out)


def third_kernel(flags, own, other, integrals, crossed, out):
    here = jnp.where(flags[1] == 0, 1.0, 0.0)
    code(product(2, own, other, integrals) + decode(crossed) * here, out)


def last_kernel(index, flags, own, other, integrals, crossed, arrived, occ_here, occ_there, vir_sum, out):
    chunk, width = out.shape
    here = jnp.where(flags[1] == 1, 1.0, 0.0)
    total = product(0, own, other, integrals) + decode(arrived) + decode(crossed) * here
    part = pl.ds(index * chunk, chunk)
    occ_rows = jnp.where(flags[0] == 0, occ_here[:, part], occ_there[:, part])
    occ_down = jnp.broadcast_to(occ_rows, (LANES, chunk)).T
    for lane in range(0, width, LANES):
        denom = vir_sum[:, lane : lane + LANES] - occ_down
        out[:, lane : lane + LANES] = (total[:, lane : lane + LANES] / denom).astype(jnp.bfloat16)


def place_kernel(index, flags, partner, own, other, *refs):
    out = refs[-1]
    rows, width = out.shape
    chunk = own.shape[0]
    upper = flags[0]
    here = upper * (rows // 2) + index * chunk
    there = (1 - upper) * (rows // 2) + index * chunk
    opposite = exchanged(other[...].astype(jnp.float32)).astype(jnp.bfloat16)

    @pl.when(upper == 0)
    def _():
        if index:
            out[...] = refs[0][...]
        out[pl.ds(pl.multiple_of(here, chunk), chunk), :] = own[...]
        out[pl.ds(pl.multiple_of(there, chunk), chunk), :] = opposite

    @pl.when(upper == 1)
    def _():
        block = 256
        lanes = lax.broadcasted_iota(jnp.int32, (block, LANES), 1) + flags[2]

        def pick(slots, begin):
            parts = [jnp.where(slots == lanes + (begin + lane), 1.0, 0.0) for lane in range(0, chunk, LANES)]
            return jnp.concatenate(parts, axis=1).astype(jnp.bfloat16)

        for begin in range(0, rows, block):
            part = pl.ds(begin, block)
            slots = jnp.broadcast_to(partner[:, part], (LANES, block)).T
            found = jnp.dot(pick(slots, here), own[...], preferred_element_type=jnp.float32)
            found += jnp.dot(pick(slots, there), opposite, preferred_element_type=jnp.float32)
            if index:
                found += refs[0][part, :].astype(jnp.float32)
            out[part, :] = found.astype(jnp.bfloat16)


def split_index(values, count):
    high = jnp.floor((values.astype(jnp.float32) + 0.5) * (1.0 / count)).astype(jnp.int32)
    return high, values - high * count


def lookup(table, positions):
    found = jnp.zeros(positions.shape, jnp.float32)
    for begin in range(0, table.shape[1], LANES):
        size = min(LANES, table.shape[1] - begin)
        part = jnp.broadcast_to(table[:, begin : begin + size], (size, size))
        down = lax.broadcasted_iota(jnp.int32, (size, size), 0)
        across = lax.broadcasted_iota(jnp.int32, (size, size), 1)
        column = jnp.sum(jnp.where(down == across, part, 0.0), axis=1, keepdims=True)
        entry = begin + lax.broadcasted_iota(jnp.int32, (size, positions.shape[1]), 0)
        found += jnp.sum(jnp.where(entry == positions, column, 0.0), axis=0, keepdims=True)
    return found


def energy_kernel(flags, pair_index, occ_energy, vir_energy, occ_lower, occ_upper, vir_sum):
    half = occ_lower.shape[1]
    for out, begin in ((occ_lower, 0), (occ_upper, half)):
        first, second = split_index(pair_index[:, pl.ds(begin, half)], NOCC)
        out[...] = lookup(occ_energy[...], first) + lookup(occ_energy[...], second)
    width = vir_sum.shape[1]
    unordered = flags[3] * (width // 2) + lax.broadcasted_iota(jnp.int32, (1, width), 1) // 2
    first, second = split_index(unordered, NV)
    vir_sum[...] = lookup(vir_energy[...], first) + lookup(vir_energy[...], second)


def across_rows(value):
    count = lax.axis_size("row")
    return lax.ppermute(value, "row", [(i, i ^ (count // 2)) for i in range(count)])


def across_pair(value):
    return lax.ppermute(value, "col", [(i, i ^ 1) for i in range(lax.axis_size("col"))])


def two_along(value):
    count = lax.axis_size("col")
    return lax.ppermute(value, "col", [(i, (i + 2) % count) for i in range(count)])


def shards(amplitudes, integrals, pair_index, partner, occ_energy, vir_energy):
    rows, width = amplitudes.shape
    half = rows // 2
    chunk = half // CHUNKS
    row_count = lax.axis_size("row")
    row = lax.axis_index("row")
    upper = (row // (row_count // 2)).astype(jnp.int32)
    col = lax.axis_index("col").astype(jnp.int32)
    odd = col % 2
    partner_base = ((row ^ (row_count // 2)) * rows).astype(jnp.int32)
    flags = jnp.stack([upper, odd, partner_base, col])

    chunk_shape = jax.ShapeDtypeStruct((chunk, width), jnp.bfloat16)
    coded_shape = jax.ShapeDtypeStruct((chunk + SCALE_ROWS, width), jnp.int16)
    whole_shape = jax.ShapeDtypeStruct((rows, width), jnp.bfloat16)

    def align(wanted, after=()):
        return call(
            functools.partial(align_kernel, wanted),
            [chunk_shape] * len(wanted),
            (flags, partner[None, :], amplitudes),
            after,
        )

    half_shape = jax.ShapeDtypeStruct((1, half), jnp.float32)
    energy_shapes = [half_shape, half_shape, jax.ShapeDtypeStruct((1, width), jnp.float32)]

    own, other, moved, crossed, arrived, done, placed = {}, {}, {}, {}, {}, {}, ()
    last = ()
    for step, index in ORDER:
        if step == "align":
            wanted = [(begin * chunk, send) for begin, send in ALIGNED[index]]
            result = align(wanted, last)
            for (begin, send), picked in zip(ALIGNED[index], result):
                if send:
                    other[begin] = across_rows(picked)
                else:
                    own[begin] = picked
            last = result[:1]
            continue
        if step == "energy":
            occ_lower, occ_upper, vir_sum = call(
                energy_kernel,
                energy_shapes,
                (flags, pair_index[None, :], occ_energy[None, :], vir_energy[None, :]),
                last,
            )
            occ_there = across_rows(occ_upper)
            last = (vir_sum,)
            continue
        inputs = (flags, own[index], other[index], integrals)
        if step == "first":
            result = call(first_kernel, coded_shape, inputs, last)
            moved[index] = two_along(result)
        elif step == "second":
            result = call(second_kernel, coded_shape, (*inputs, moved[index]), last)
            crossed[index] = across_pair(result)
        elif step == "third":
            result = call(third_kernel, coded_shape, (*inputs, crossed[index]), last)
            arrived[index] = two_along(result)
        elif step == "last":
            sums = (crossed[index], arrived[index], occ_lower, occ_there, vir_sum)
            result = call(functools.partial(last_kernel, index), chunk_shape, (*inputs, *sums), last)
            done[index] = (result, across_rows(result))
        else:
            ready = (flags, partner[None, :], *done[index], *placed)
            result = call(functools.partial(place_kernel, index), whole_shape, ready, last)
            placed = (result,)
        last = (result,)
    return result


def solution(mesh):
    in_specs = (P("row", "col"), P("col", None), P("row"), P("row"), P(), P())
    out_specs = P("row", "col")
    return jax.shard_map(shards, mesh=mesh, in_specs=in_specs, out_specs=out_specs, check_vma=False)
```

```python
import functools

import jax
import jax.numpy as jnp
from jax import lax
from jax.experimental import pallas as pl
from jax.experimental.pallas import tpu as pltpu
from jax.sharding import PartitionSpec as P

NOCC = 200
NV = 2000
CHUNKS = 4
SCALE_ROWS = 16
TOP = 32767.0
STEPS = 64.0
TINY = 1e-33
LANES = 128
VMEM_LIMIT = 8 * 1024 * 1024
KERNEL_FLOPS = 4 * 10**9
ORDER = (
    (("align", 0), ("align", 1), ("energy", 0), ("first", 0), ("align", 2), ("first", 1))
    + (("align", 3), ("first", 2), ("second", 0), ("second", 1), ("first", 3), ("third", 0))
    + (("second", 2), ("third", 1), ("second", 3), ("third", 2), ("last", 0), ("third", 3))
    + (("last", 1), ("last", 2), ("place", 0), ("last", 3), ("place", 1), ("place", 2))
    + (("place", 3),)
)
ALIGNED = (
    ((0, True),),
    ((1, True), (0, False)),
    ((2, True), (1, False)),
    ((3, True), (2, False), (3, False)),
)

VMEM = pl.BlockSpec(memory_space=pltpu.VMEM)
SMEM = pl.BlockSpec(memory_space=pltpu.SMEM)
ANY = pl.BlockSpec(memory_space=pl.ANY)


def call(body, out_shape, operands, after=()):
    count = len(operands)

    def kernel(*refs):
        body(*refs[:count], *refs[count + len(after) :])

    return pl.pallas_call(
        kernel,
        out_shape=out_shape,
        in_specs=[SMEM] + [VMEM] * (count - 1) + [ANY] * len(after),
        out_specs=jax.tree.map(lambda _: VMEM, out_shape),
        compiler_params=pltpu.CompilerParams(vmem_limit_bytes=VMEM_LIMIT),
        cost_estimate=pl.CostEstimate(flops=KERNEL_FLOPS, bytes_accessed=1, transcendentals=0),
    )(*operands, *after)


def exchanged(values):
    even = lax.broadcasted_iota(jnp.int32, (values.shape[0], LANES), 1) % 2 == 0
    parts = []
    for lane in range(0, values.shape[1], LANES):
        part = values[:, lane : lane + LANES]
        parts.append(jnp.where(even, pltpu.roll(part, LANES - 1, 1), pltpu.roll(part, 1, 1)))
    return jnp.concatenate(parts, axis=1)


def align_kernel(wanted, flags, partner, amplitudes, *outs):
    rows = amplitudes.shape[0]
    chunk = outs[0].shape[0]
    upper = flags[0]

    def first(index):
        begin, send = wanted[index]
        return (1 - upper if send else upper) * (rows // 2) + begin

    @pl.when(upper == 0)
    def _():
        for index, out in enumerate(outs):
            out[...] = amplitudes[pl.ds(pl.multiple_of(first(index), chunk), chunk), :]

    @pl.when(upper == 1)
    def _():
        for index, out in enumerate(outs):
            target = flags[2] + first(index) + lax.broadcasted_iota(jnp.int32, (chunk, rows), 0)
            pick = jnp.where(partner[...] == target, 1.0, 0.0).astype(jnp.bfloat16)
            out[...] = jnp.dot(pick, amplitudes[...], preferred_element_type=jnp.float32).astype(jnp.bfloat16)


def product(stop, own, other, integrals):
    factor = integrals[:, pl.ds(stop * own.shape[1], own.shape[1])]
    direct = jnp.dot(own[...], factor, preferred_element_type=jnp.float32)
    return direct + exchanged(jnp.dot(other[...], factor, preferred_element_type=jnp.float32))


def code(values, out):
    rows = values.shape[0]
    top = jnp.max(jnp.abs(values), axis=0, keepdims=True)
    level = jnp.ceil(STEPS * jnp.log2(jnp.maximum(top, TINY) * (1.0001 / TOP)))
    coded = jnp.round(values * jnp.exp2(level * (-1.0 / STEPS)))
    out[pl.ds(0, rows), :] = coded.astype(jnp.int32).astype(jnp.int16)
    spread = jnp.broadcast_to(level.astype(jnp.int32), (SCALE_ROWS, values.shape[1]))
    out[pl.ds(rows, SCALE_ROWS), :] = spread.astype(jnp.int16)


def decode(coded):
    rows = coded.shape[0] - SCALE_ROWS
    level = coded[pl.ds(rows, SCALE_ROWS), :].astype(jnp.int32).astype(jnp.float32)[0:1, :]
    return coded[pl.ds(0, rows), :].astype(jnp.int32).astype(jnp.float32) * jnp.exp2(level * (1.0 / STEPS))


def first_kernel(flags, own, other, integrals, out):
    code(product(3, own, other, integrals), out)


def second_kernel(flags, own, other, integrals, arrived, out):
    code(product(1, own, other, integrals) + decode(arrived), out)


def third_kernel(flags, own, other, integrals, crossed, out):
    here = jnp.where(flags[1] == 0, 1.0, 0.0)
    code(product(2, own, other, integrals) + decode(crossed) * here, out)


def last_kernel(index, flags, own, other, integrals, crossed, arrived, occ_here, occ_there, vir_sum, out):
    chunk, width = out.shape
    here = jnp.where(flags[1] == 1, 1.0, 0.0)
    total = product(0, own, other, integrals) + decode(arrived) + decode(crossed) * here
    part = pl.ds(index * chunk, chunk)
    occ_rows = jnp.where(flags[0] == 0, occ_here[:, part], occ_there[:, part])
    occ_down = jnp.broadcast_to(occ_rows, (LANES, chunk)).T
    for lane in range(0, width, LANES):
        denom = vir_sum[:, lane : lane + LANES] - occ_down
        out[:, lane : lane + LANES] = (total[:, lane : lane + LANES] / denom).astype(jnp.bfloat16)


def place_kernel(index, flags, partner, own, other, *refs):
    out = refs[-1]
    rows, width = out.shape
    chunk = own.shape[0]
    upper = flags[0]
    here = upper * (rows // 2) + index * chunk
    there = (1 - upper) * (rows // 2) + index * chunk
    opposite = exchanged(other[...].astype(jnp.float32)).astype(jnp.bfloat16)

    @pl.when(upper == 0)
    def _():
        if index:
            out[...] = refs[0][...]
        out[pl.ds(pl.multiple_of(here, chunk), chunk), :] = own[...]
        out[pl.ds(pl.multiple_of(there, chunk), chunk), :] = opposite

    @pl.when(upper == 1)
    def _():
        block = 256
        lanes = lax.broadcasted_iota(jnp.int32, (block, LANES), 1) + flags[2]

        def pick(slots, begin):
            parts = [jnp.where(slots == lanes + (begin + lane), 1.0, 0.0) for lane in range(0, chunk, LANES)]
            return jnp.concatenate(parts, axis=1).astype(jnp.bfloat16)

        for begin in range(0, rows, block):
            part = pl.ds(begin, block)
            slots = jnp.broadcast_to(partner[:, part], (LANES, block)).T
            found = jnp.dot(pick(slots, here), own[...], preferred_element_type=jnp.float32)
            found += jnp.dot(pick(slots, there), opposite, preferred_element_type=jnp.float32)
            if index:
                found += refs[0][part, :].astype(jnp.float32)
            out[part, :] = found.astype(jnp.bfloat16)


def split_index(values, count):
    high = jnp.floor((values.astype(jnp.float32) + 0.5) * (1.0 / count)).astype(jnp.int32)
    return high, values - high * count


def lookup(table, positions):
    found = jnp.zeros(positions.shape, jnp.float32)
    for begin in range(0, table.shape[1], LANES):
        size = min(LANES, table.shape[1] - begin)
        part = jnp.broadcast_to(table[:, begin : begin + size], (size, size))
        down = lax.broadcasted_iota(jnp.int32, (size, size), 0)
        across = lax.broadcasted_iota(jnp.int32, (size, size), 1)
        column = jnp.sum(jnp.where(down == across, part, 0.0), axis=1, keepdims=True)
        entry = begin + lax.broadcasted_iota(jnp.int32, (size, positions.shape[1]), 0)
        found += jnp.sum(jnp.where(entry == positions, column, 0.0), axis=0, keepdims=True)
    return found


def energy_kernel(flags, pair_index, occ_energy, vir_energy, occ_lower, occ_upper, vir_sum):
    half = occ_lower.shape[1]
    for out, begin in ((occ_lower, 0), (occ_upper, half)):
        first, second = split_index(pair_index[:, pl.ds(begin, half)], NOCC)
        out[...] = lookup(occ_energy[...], first) + lookup(occ_energy[...], second)
    width = vir_sum.shape[1]
    unordered = flags[3] * (width // 2) + lax.broadcasted_iota(jnp.int32, (1, width), 1) // 2
    first, second = split_index(unordered, NV)
    vir_sum[...] = lookup(vir_energy[...], first) + lookup(vir_energy[...], second)


def across_rows(value):
    count = lax.axis_size("row")
    return lax.ppermute(value, "row", [(i, i ^ (count // 2)) for i in range(count)])


def across_pair(value):
    return lax.ppermute(value, "col", [(i, i ^ 1) for i in range(lax.axis_size("col"))])


def two_along(value):
    count = lax.axis_size("col")
    return lax.ppermute(value, "col", [(i, (i + 2) % count) for i in range(count)])


def shards(amplitudes, integrals, pair_index, partner, occ_energy, vir_energy):
    rows, width = amplitudes.shape
    half = rows // 2
    chunk = half // CHUNKS
    row_count = lax.axis_size("row")
    row = lax.axis_index("row")
    upper = (row // (row_count // 2)).astype(jnp.int32)
    col = lax.axis_index("col").astype(jnp.int32)
    odd = col % 2
    partner_base = ((row ^ (row_count // 2)) * rows).astype(jnp.int32)
    flags = jnp.stack([upper, odd, partner_base, col])

    chunk_shape = jax.ShapeDtypeStruct((chunk, width), jnp.bfloat16)
    coded_shape = jax.ShapeDtypeStruct((chunk + SCALE_ROWS, width), jnp.int16)
    whole_shape = jax.ShapeDtypeStruct((rows, width), jnp.bfloat16)

    def align(wanted, after=()):
        return call(
            functools.partial(align_kernel, wanted),
            [chunk_shape] * len(wanted),
            (flags, partner[None, :], amplitudes),
            after,
        )

    half_shape = jax.ShapeDtypeStruct((1, half), jnp.float32)
    energy_shapes = [half_shape, half_shape, jax.ShapeDtypeStruct((1, width), jnp.float32)]

    own, other, moved, crossed, arrived, done, placed = {}, {}, {}, {}, {}, {}, ()
    last = ()
    for step, index in ORDER:
        if step == "align":
            wanted = [(begin * chunk, send) for begin, send in ALIGNED[index]]
            result = align(wanted, last)
            for (begin, send), picked in zip(ALIGNED[index], result):
                if send:
                    other[begin] = across_rows(picked)
                else:
                    own[begin] = picked
            last = result[:1]
            continue
        if step == "energy":
            occ_lower, occ_upper, vir_sum = call(
                energy_kernel,
                energy_shapes,
                (flags, pair_index[None, :], occ_energy[None, :], vir_energy[None, :]),
                last,
            )
            occ_there = across_rows(occ_upper)
            last = (vir_sum,)
            continue
        inputs = (flags, own[index], other[index], integrals)
        if step == "first":
            result = call(first_kernel, coded_shape, inputs, last)
            moved[index] = two_along(result)
        elif step == "second":
            result = call(second_kernel, coded_shape, (*inputs, moved[index]), last)
            crossed[index] = across_pair(result)
        elif step == "third":
            result = call(third_kernel, coded_shape, (*inputs, crossed[index]), last)
            arrived[index] = two_along(result)
        elif step == "last":
            sums = (crossed[index], arrived[index], occ_lower, occ_there, vir_sum)
            result = call(functools.partial(last_kernel, index), chunk_shape, (*inputs, *sums), last)
            done[index] = (result, across_rows(result))
        else:
            ready = (flags, partner[None, :], *done[index], *placed)
            result = call(functools.partial(place_kernel, index), whole_shape, ready, last)
            placed = (result,)
        last = (result,)
    return result


def solution(mesh):
    in_specs = (P("row", "col"), P("col", None), P("row"), P("row"), P(), P())
    out_specs = P("row", "col")
    return jax.shard_map(shards, mesh=mesh, in_specs=in_specs, out_specs=out_specs, check_vma=False)
```

```python
import functools

import jax
import jax.numpy as jnp
from jax import lax
from jax.experimental import pallas as pl
from jax.experimental.pallas import tpu as pltpu
from jax.sharding import PartitionSpec as P

NOCC = 200
NV = 2000
SHARES = (2, 2, 2, 2)
SCALE_ROWS = 16
TOP = 32767.0
STEPS = 64.0
TINY = 1e-33
LANES = 128
PLACE_ROWS = 256
VMEM_LIMIT = 16 * 1024 * 1024
KERNEL_FLOPS = 4 * 10**9
ORDER = (
    (("align", 0), ("align", 1), ("factor", 0), ("energy", 0), ("first", 0), ("align", 2))
    + (("first", 1), ("align", 3), ("first", 2), ("second", 0), ("second", 1), ("first", 3))
    + (("third", 0), ("second", 2), ("third", 1), ("second", 3), ("third", 2), ("last", 0))
    + (("third", 3), ("last", 1), ("last", 2), ("place", 0), ("last", 3), ("place", 1))
    + (("place", 2), ("place", 3))
)
ALIGNED = (
    ((0, True),),
    ((1, True), (0, False)),
    ((2, True), (1, False)),
    ((3, True), (2, False), (3, False)),
)

VMEM = pl.BlockSpec(memory_space=pltpu.VMEM)
ANY = pl.BlockSpec(memory_space=pl.ANY)


def call(body, out_shape, operands, after=(), out_spec=None, scratch=()):
    count = len(operands)

    def kernel(*refs):
        body(*refs[:count], *refs[count + len(after) :])

    return pl.pallas_call(
        kernel,
        out_shape=out_shape,
        in_specs=[VMEM] * count + [ANY] * len(after),
        out_specs=jax.tree.map(lambda _: out_spec or VMEM, out_shape),
        scratch_shapes=list(scratch),
        compiler_params=pltpu.CompilerParams(vmem_limit_bytes=VMEM_LIMIT),
        cost_estimate=pl.CostEstimate(flops=KERNEL_FLOPS, bytes_accessed=1, transcendentals=0),
    )(*operands, *after)


def upper_side():
    return lax.axis_index("row") // (lax.axis_size("row") // 2)


def partner_base(rows):
    return (lax.axis_index("row") ^ (lax.axis_size("row") // 2)) * rows


def exchanged(values):
    even = lax.broadcasted_iota(jnp.int32, (values.shape[0], LANES), 1) % 2 == 0
    parts = []
    for lane in range(0, values.shape[1], LANES):
        part = values[:, lane : lane + LANES]
        parts.append(jnp.where(even, pltpu.roll(part, LANES - 1, 1), pltpu.roll(part, 1, 1)))
    return jnp.concatenate(parts, axis=1)


def align_kernel(wanted, partner, amplitudes, *outs):
    rows = amplitudes.shape[0]
    upper = upper_side()

    def first(index):
        begin, send = wanted[index]
        return (1 - upper if send else upper) * (rows // 2) + begin

    @pl.when(upper == 0)
    def _():
        for index, out in enumerate(outs):
            out[...] = amplitudes[pl.ds(pl.multiple_of(first(index), LANES), out.shape[0]), :]

    @pl.when(upper == 1)
    def _():
        for index, out in enumerate(outs):
            target = partner_base(rows) + first(index) + lax.broadcasted_iota(jnp.int32, (out.shape[0], rows), 0)
            pick = jnp.where(partner[...] == target, 1.0, 0.0).astype(jnp.bfloat16)
            out[...] = jnp.dot(pick, amplitudes[...], preferred_element_type=jnp.float32).astype(jnp.bfloat16)


def factor_kernel(integrals, *outs):
    width = integrals.shape[0]
    for stop, out in enumerate(outs):
        block = integrals[:, pl.ds(stop * width, width)]
        out[pl.ds(0, width), :] = block
        out[pl.ds(width, width), :] = exchanged(block.astype(jnp.float32)).astype(jnp.bfloat16)


def product(own, other, factor):
    both = jnp.concatenate([own[...], other[...]], axis=1)
    return jnp.dot(both, factor[...], preferred_element_type=jnp.float32)


def code(values, out):
    rows = values.shape[0]
    top = jnp.max(jnp.abs(values), axis=0, keepdims=True)
    level = jnp.ceil(STEPS * jnp.log2(jnp.maximum(top, TINY) * (1.0001 / TOP)))
    coded = jnp.round(values * jnp.exp2(level * (-1.0 / STEPS)))
    out[pl.ds(0, rows), :] = coded.astype(jnp.int32).astype(jnp.int16)
    spread = jnp.broadcast_to(level.astype(jnp.int32), (SCALE_ROWS, values.shape[1]))
    out[pl.ds(rows, SCALE_ROWS), :] = spread.astype(jnp.int16)


def decode(coded):
    rows = coded.shape[0] - SCALE_ROWS
    level = coded[pl.ds(rows, SCALE_ROWS), :].astype(jnp.int32).astype(jnp.float32)[0:1, :]
    return coded[pl.ds(0, rows), :].astype(jnp.int32).astype(jnp.float32) * jnp.exp2(level * (1.0 / STEPS))


def first_kernel(own, other, factor, out):
    code(product(own, other, factor), out)


def second_kernel(own, other, factor, arrived, out):
    code(product(own, other, factor) + decode(arrived), out)


def third_kernel(own, other, factor, crossed, out):
    here = jnp.where(lax.axis_index("col") % 2 == 0, 1.0, 0.0)
    code(product(own, other, factor) + decode(crossed) * here, out)


def last_kernel(begin, own, other, factor, crossed, arrived, occ_here, occ_there, vir_sum, out):
    chunk, width = out.shape
    here = jnp.where(lax.axis_index("col") % 2 == 1, 1.0, 0.0)
    total = product(own, other, factor) + decode(arrived) + decode(crossed) * here
    part = pl.ds(begin, chunk)
    occ_rows = jnp.where(upper_side() == 0, occ_here[:, part], occ_there[:, part])
    occ_down = jnp.broadcast_to(occ_rows, (LANES, chunk)).T
    for lane in range(0, width, LANES):
        denom = vir_sum[:, lane : lane + LANES] - occ_down
        out[:, lane : lane + LANES] = (total[:, lane : lane + LANES] / denom).astype(jnp.bfloat16)


def place_kernel(begin, partner, own, other, *refs):
    held, arrivals = refs[-2:] if len(refs) > 2 else (refs[-1], None)
    earlier = refs[0] if len(refs) != 1 else None
    rows, width = held.shape
    chunk = own.shape[0]
    upper = upper_side()
    here = upper * (rows // 2) + begin
    there = (1 - upper) * (rows // 2) + begin
    opposite = exchanged(other[...].astype(jnp.float32)).astype(jnp.bfloat16)

    def leave(block):
        part = pl.ds(block * PLACE_ROWS, PLACE_ROWS)
        return pltpu.make_async_copy(held.at[part, :], refs[-3].at[part, :], arrivals.at[block])

    @pl.when(upper == 0)
    def _():
        if earlier is not None:
            held[...] = earlier[...]
        held[pl.ds(pl.multiple_of(here, LANES), chunk), :] = own[...]
        held[pl.ds(pl.multiple_of(there, LANES), chunk), :] = opposite
        if arrivals is not None:
            for block in range(rows // PLACE_ROWS):
                leave(block).start()

    @pl.when(upper == 1)
    def _():
        lanes = lax.broadcasted_iota(jnp.int32, (PLACE_ROWS, LANES), 1) + partner_base(rows)

        def pick(slots, begin):
            parts = [jnp.where(slots == lanes + (begin + lane), 1.0, 0.0) for lane in range(0, chunk, LANES)]
            return jnp.concatenate(parts, axis=1).astype(jnp.bfloat16)

        for block in range(rows // PLACE_ROWS):
            part = pl.ds(block * PLACE_ROWS, PLACE_ROWS)
            slots = jnp.broadcast_to(partner[:, part], (LANES, PLACE_ROWS)).T
            found = jnp.dot(pick(slots, here), own[...], preferred_element_type=jnp.float32)
            found += jnp.dot(pick(slots, there), opposite, preferred_element_type=jnp.float32)
            if earlier is not None:
                found += earlier[part, :].astype(jnp.float32)
            held[part, :] = found.astype(jnp.bfloat16)
            if arrivals is not None:
                leave(block).start()

    if arrivals is not None:
        for block in range(rows // PLACE_ROWS):
            leave(block).wait()


def split_index(values, count):
    high = jnp.floor((values.astype(jnp.float32) + 0.5) * (1.0 / count)).astype(jnp.int32)
    return high, values - high * count


def lookup(table, positions):
    found = jnp.zeros(positions.shape, jnp.float32)
    for begin in range(0, table.shape[1], LANES):
        size = min(LANES, table.shape[1] - begin)
        part = jnp.broadcast_to(table[:, begin : begin + size], (size, size))
        down = lax.broadcasted_iota(jnp.int32, (size, size), 0)
        across = lax.broadcasted_iota(jnp.int32, (size, size), 1)
        column = jnp.sum(jnp.where(down == across, part, 0.0), axis=1, keepdims=True)
        entry = begin + lax.broadcasted_iota(jnp.int32, (size, positions.shape[1]), 0)
        found += jnp.sum(jnp.where(entry == positions, column, 0.0), axis=0, keepdims=True)
    return found


def energy_kernel(pair_index, occ_energy, vir_energy, occ_lower, occ_upper, vir_sum):
    half = occ_lower.shape[1]
    for out, begin in ((occ_lower, 0), (occ_upper, half)):
        first, second = split_index(pair_index[:, pl.ds(begin, half)], NOCC)
        out[...] = lookup(occ_energy[...], first) + lookup(occ_energy[...], second)
    width = vir_sum.shape[1]
    unordered = lax.axis_index("col") * (width // 2) + lax.broadcasted_iota(jnp.int32, (1, width), 1) // 2
    first, second = split_index(unordered, NV)
    vir_sum[...] = lookup(vir_energy[...], first) + lookup(vir_energy[...], second)


def across_rows(value):
    count = lax.axis_size("row")
    return lax.ppermute(value, "row", [(i, i ^ (count // 2)) for i in range(count)])


def across_pair(value):
    return lax.ppermute(value, "col", [(i, i ^ 1) for i in range(lax.axis_size("col"))])


def two_along(value):
    count = lax.axis_size("col")
    return lax.ppermute(value, "col", [(i, (i + 2) % count) for i in range(count)])


def shards(amplitudes, integrals, pair_index, partner, occ_energy, vir_energy):
    rows, width = amplitudes.shape
    half = rows // 2
    chunks = [half * share // sum(SHARES) for share in SHARES]
    begins = [sum(chunks[:index]) for index in range(len(chunks))]
    whole_shape = jax.ShapeDtypeStruct((rows, width), jnp.bfloat16)

    def chunk_shape(index):
        return jax.ShapeDtypeStruct((chunks[index], width), jnp.bfloat16)

    def coded_shape(index):
        return jax.ShapeDtypeStruct((chunks[index] + SCALE_ROWS, width), jnp.int16)

    half_shape = jax.ShapeDtypeStruct((1, half), jnp.float32)
    energy_shapes = [half_shape, half_shape, jax.ShapeDtypeStruct((1, width), jnp.float32)]

    own, other, moved, crossed, arrived, done, placed = {}, {}, {}, {}, {}, {}, ()
    last = ()
    for step, index in ORDER:
        if step == "align":
            wanted = tuple((begins[chunk], send) for chunk, send in ALIGNED[index])
            shapes = [chunk_shape(chunk) for chunk, _ in ALIGNED[index]]
            result = call(functools.partial(align_kernel, wanted), shapes, (partner[None, :], amplitudes), last)
            for (chunk, send), picked in zip(ALIGNED[index], result):
                if send:
                    other[chunk] = across_rows(picked)
                else:
                    own[chunk] = picked
            last = result[:1]
            continue
        if step == "factor":
            shapes = [jax.ShapeDtypeStruct((2 * width, width), jnp.bfloat16)] * 4
            factors = call(factor_kernel, shapes, (integrals,), last)
            last = factors[:1]
            continue
        if step == "energy":
            occ_lower, occ_upper, vir_sum = call(
                energy_kernel,
                energy_shapes,
                (pair_index[None, :], occ_energy[None, :], vir_energy[None, :]),
                last,
            )
            occ_there = across_rows(occ_upper)
            last = (vir_sum,)
            continue
        inputs = (own[index], other[index])
        if step == "first":
            result = call(first_kernel, coded_shape(index), (*inputs, factors[3]), last)
            moved[index] = two_along(result)
        elif step == "second":
            result = call(second_kernel, coded_shape(index), (*inputs, factors[1], moved[index]), last)
            crossed[index] = across_pair(result)
        elif step == "third":
            result = call(third_kernel, coded_shape(index), (*inputs, factors[2], crossed[index]), last)
            arrived[index] = two_along(result)
        elif step == "last":
            sums = (crossed[index], arrived[index], occ_lower, occ_there, vir_sum)
            result = call(functools.partial(last_kernel, begins[index]), chunk_shape(index), (*inputs, factors[0], *sums), last)
            done[index] = (result, across_rows(result))
        else:
            ready = (partner[None, :], *done[index], *placed)
            final = {}
            if (step, index) == ORDER[-1]:
                blocks = pltpu.SemaphoreType.DMA((rows // PLACE_ROWS,))
                final = {"out_spec": ANY, "scratch": (pltpu.VMEM((rows, width), jnp.bfloat16), blocks)}
            result = call(functools.partial(place_kernel, begins[index]), whole_shape, ready, last, **final)
            placed = (result,)
        last = (result,)
    return result


def solution(mesh):
    in_specs = (P("row", "col"), P("col", None), P("row"), P("row"), P(), P())
    out_specs = P("row", "col")
    return jax.shard_map(shards, mesh=mesh, in_specs=in_specs, out_specs=out_specs, check_vma=False)
```

```python
import functools

import jax
import jax.numpy as jnp
from jax import lax
from jax.experimental import pallas as pl
from jax.experimental.pallas import tpu as pltpu
from jax.sharding import PartitionSpec as P

NOCC = 200
NV = 2000
SHARES = (2, 2, 2, 2)
SCALE_ROWS = 16
TOP = 32767.0
STEPS = 64.0
TINY = 1e-33
LANES = 128
PLACE_ROWS = 256
VMEM_LIMIT = 16 * 1024 * 1024
KERNEL_FLOPS = 4 * 10**9
ORDER = (
    (("align", 1), ("factor", 0), ("energy", 0), ("first", 0), ("align", 2), ("first", 1))
    + (("align", 3), ("first", 2), ("second", 0), ("second", 1), ("first", 3), ("third", 0))
    + (("second", 2), ("second", 3), ("third", 1), ("third", 2), ("last", 0), ("third", 3))
    + (("last", 1), ("last", 2), ("last", 3), ("place", 0), ("place", 1), ("place", 2))
)
ALIGNED = (
    (),
    ((1, True), (0, False)),
    ((2, True), (1, False)),
    ((3, True), (2, False), (3, False)),
)

VMEM = pl.BlockSpec(memory_space=pltpu.VMEM)
HBM = pl.BlockSpec(memory_space=pltpu.HBM)
ANY = pl.BlockSpec(memory_space=pl.ANY)


def call(body, out_shape, operands, after=(), in_spec=None, out_spec=None, scratch=()):
    count = len(operands)

    def kernel(*refs):
        body(*refs[:count], *refs[count + len(after) :])

    return pl.pallas_call(
        kernel,
        out_shape=out_shape,
        in_specs=[in_spec or VMEM] * count + [ANY] * len(after),
        out_specs=jax.tree.map(lambda _: out_spec or VMEM, out_shape),
        scratch_shapes=list(scratch),
        compiler_params=pltpu.CompilerParams(vmem_limit_bytes=VMEM_LIMIT),
        cost_estimate=pl.CostEstimate(flops=KERNEL_FLOPS, bytes_accessed=1, transcendentals=0),
    )(*operands, *after)


def upper_side():
    return lax.axis_index("row") // (lax.axis_size("row") // 2)


def partner_base(rows):
    return (lax.axis_index("row") ^ (lax.axis_size("row") // 2)) * rows


def exchanged(values):
    even = lax.broadcasted_iota(jnp.int32, (values.shape[0], LANES), 1) % 2 == 0
    parts = []
    for lane in range(0, values.shape[1], LANES):
        part = values[:, lane : lane + LANES]
        parts.append(jnp.where(even, pltpu.roll(part, LANES - 1, 1), pltpu.roll(part, 1, 1)))
    return jnp.concatenate(parts, axis=1)


def align_kernel(wanted, partner, amplitudes, *outs):
    rows = amplitudes.shape[0]
    upper = upper_side()

    def first(index):
        begin, send = wanted[index]
        return (1 - upper if send else upper) * (rows // 2) + begin

    @pl.when(upper == 0)
    def _():
        for index, out in enumerate(outs):
            out[...] = amplitudes[pl.ds(pl.multiple_of(first(index), LANES), out.shape[0]), :]

    @pl.when(upper == 1)
    def _():
        for index, out in enumerate(outs):
            target = partner_base(rows) + first(index) + lax.broadcasted_iota(jnp.int32, (out.shape[0], rows), 0)
            pick = jnp.where(partner[...] == target, 1.0, 0.0).astype(jnp.bfloat16)
            out[...] = jnp.dot(pick, amplitudes[...], preferred_element_type=jnp.float32).astype(jnp.bfloat16)


def align_first_kernel(partner, amplitudes, out, held, slots, arrivals):
    rows, chunk = amplitudes.shape[0], out.shape[0]
    upper = upper_side()
    first = (1 - upper) * (rows // 2)
    blocks = rows // chunk

    def fetch(block):
        part = pl.ds(block * chunk, chunk)
        return pltpu.make_async_copy(amplitudes.at[part, :], held.at[part, :], arrivals.at[block])

    @pl.when(upper == 0)
    def _():
        part = pl.ds(pl.multiple_of(first, LANES), chunk)
        straight = pltpu.make_async_copy(amplitudes.at[part, :], out, arrivals.at[0])
        straight.start()
        straight.wait()

    @pl.when(upper == 1)
    def _():
        slots_copy = pltpu.make_async_copy(partner, slots, arrivals.at[blocks])
        slots_copy.start()
        for block in range(blocks):
            fetch(block).start()
        slots_copy.wait()
        target = partner_base(rows) + first + lax.broadcasted_iota(jnp.int32, (chunk, chunk), 0)
        total = jnp.zeros(out.shape, jnp.float32)
        for block in range(blocks):
            part = pl.ds(block * chunk, chunk)
            pick = jnp.where(slots[:, part] == target, 1.0, 0.0).astype(jnp.bfloat16)
            fetch(block).wait()
            total += jnp.dot(pick, held[part, :], preferred_element_type=jnp.float32)
        out[...] = total.astype(jnp.bfloat16)


def factor_kernel(integrals, *outs):
    width = integrals.shape[0]
    for stop, out in enumerate(outs):
        block = integrals[:, pl.ds(stop * width, width)]
        out[pl.ds(0, width), :] = block
        out[pl.ds(width, width), :] = exchanged(block.astype(jnp.float32)).astype(jnp.bfloat16)


def product(own, other, factor):
    both = jnp.concatenate([own[...], other[...]], axis=1)
    return jnp.dot(both, factor[...], preferred_element_type=jnp.float32)


def code(values, out):
    rows = values.shape[0]
    top = jnp.max(jnp.abs(values), axis=0, keepdims=True)
    level = jnp.ceil(STEPS * jnp.log2(jnp.maximum(top, TINY) * (1.0001 / TOP)))
    coded = jnp.round(values * jnp.exp2(level * (-1.0 / STEPS)))
    out[pl.ds(0, rows), :] = coded.astype(jnp.int32).astype(jnp.int16)
    spread = jnp.broadcast_to(level.astype(jnp.int32), (SCALE_ROWS, values.shape[1]))
    out[pl.ds(rows, SCALE_ROWS), :] = spread.astype(jnp.int16)


def decode(coded):
    rows = coded.shape[0] - SCALE_ROWS
    level = coded[pl.ds(rows, SCALE_ROWS), :].astype(jnp.int32).astype(jnp.float32)[0:1, :]
    return coded[pl.ds(0, rows), :].astype(jnp.int32).astype(jnp.float32) * jnp.exp2(level * (1.0 / STEPS))


def first_kernel(own, other, factor, out):
    code(product(own, other, factor), out)


def second_kernel(own, other, factor, arrived, out):
    code(product(own, other, factor) + decode(arrived), out)


def third_kernel(own, other, factor, crossed, out):
    here = jnp.where(lax.axis_index("col") % 2 == 0, 1.0, 0.0)
    code(product(own, other, factor) + decode(crossed) * here, out)


def last_kernel(begin, own, other, factor, crossed, arrived, occ_here, occ_there, vir_sum, out):
    chunk, width = out.shape
    here = jnp.where(lax.axis_index("col") % 2 == 1, 1.0, 0.0)
    total = product(own, other, factor) + decode(arrived) + decode(crossed) * here
    part = pl.ds(begin, chunk)
    occ_rows = jnp.where(upper_side() == 0, occ_here[:, part], occ_there[:, part])
    occ_down = jnp.broadcast_to(occ_rows, (LANES, chunk)).T
    for lane in range(0, width, LANES):
        denom = vir_sum[:, lane : lane + LANES] - occ_down
        out[:, lane : lane + LANES] = (total[:, lane : lane + LANES] / denom).astype(jnp.bfloat16)


def pick_rows(partner, block, size, begin, count):
    slots = jnp.broadcast_to(partner[:, pl.ds(block * size, size)], (LANES, size)).T
    lanes = lax.broadcasted_iota(jnp.int32, (size, LANES), 1) + (partner_base(partner.shape[1]) + begin)
    parts = [jnp.where(slots == lanes + lane, 1.0, 0.0) for lane in range(0, count, LANES)]
    return jnp.concatenate(parts, axis=1).astype(jnp.bfloat16)


def place_kernel(begin, partner, own, other, *refs):
    earlier, out = refs[:-1], refs[-1]
    rows, chunk = out.shape[0], own.shape[0]
    upper = upper_side()
    here = upper * (rows // 2) + begin
    there = (1 - upper) * (rows // 2) + begin
    opposite = exchanged(other[...].astype(jnp.float32)).astype(jnp.bfloat16)

    @pl.when(upper == 0)
    def _():
        if earlier:
            out[...] = earlier[0][...]
        out[pl.ds(pl.multiple_of(here, LANES), chunk), :] = own[...]
        out[pl.ds(pl.multiple_of(there, LANES), chunk), :] = opposite

    @pl.when(upper == 1)
    def _():
        for block in range(rows // PLACE_ROWS):
            part = pl.ds(block * PLACE_ROWS, PLACE_ROWS)
            pick = pick_rows(partner, block, PLACE_ROWS, here, chunk)
            found = jnp.dot(pick, own[...], preferred_element_type=jnp.float32)
            pick = pick_rows(partner, block, PLACE_ROWS, there, chunk)
            found += jnp.dot(pick, opposite, preferred_element_type=jnp.float32)
            if earlier:
                found += earlier[0][part, :].astype(jnp.float32)
            out[part, :] = found.astype(jnp.bfloat16)


def place_own_kernel(begin, partner, own, earlier, out, picks):
    rows, chunk = out.shape[0], own.shape[0]
    upper = upper_side()
    here = upper * (rows // 2) + begin
    there = (1 - upper) * (rows // 2) + begin

    @pl.when(upper == 0)
    def _():
        out[...] = earlier[...]
        out[pl.ds(pl.multiple_of(here, LANES), chunk), :] = own[...]

    @pl.when(upper == 1)
    def _():
        for block in range(rows // PLACE_ROWS):
            part = pl.ds(block * PLACE_ROWS, PLACE_ROWS)
            pick = pick_rows(partner, block, PLACE_ROWS, here, chunk)
            found = jnp.dot(pick, own[...], preferred_element_type=jnp.float32)
            out[part, :] = (found + earlier[part, :].astype(jnp.float32)).astype(jnp.bfloat16)
            picks[part, :] = pick_rows(partner, block, PLACE_ROWS, there, chunk)


def place_other_kernel(begin, earlier, picks, other, out, held, arrivals):
    rows, chunk = held.shape[0], other.shape[0]
    upper = upper_side()
    there = (1 - upper) * (rows // 2) + begin
    opposite = exchanged(other[...].astype(jnp.float32)).astype(jnp.bfloat16)

    def leave(block):
        part = pl.ds(block * chunk, chunk)
        return pltpu.make_async_copy(held.at[part, :], out.at[part, :], arrivals.at[block])

    @pl.when(upper == 0)
    def _():
        for block in range(rows // chunk):
            part = pl.ds(block * chunk, chunk)
            held[part, :] = jnp.where(there == block * chunk, opposite, earlier[part, :])
            leave(block).start()

    @pl.when(upper == 1)
    def _():
        for block in range(rows // chunk):
            part = pl.ds(block * chunk, chunk)
            found = jnp.dot(picks[part, :], opposite, preferred_element_type=jnp.float32)
            held[part, :] = (found + earlier[part, :].astype(jnp.float32)).astype(jnp.bfloat16)
            leave(block).start()

    for block in range(rows // chunk):
        leave(block).wait()


def split_index(values, count):
    high = jnp.floor((values.astype(jnp.float32) + 0.5) * (1.0 / count)).astype(jnp.int32)
    return high, values - high * count


def lookup(table, positions):
    found = jnp.zeros(positions.shape, jnp.float32)
    for begin in range(0, table.shape[1], LANES):
        size = min(LANES, table.shape[1] - begin)
        part = jnp.broadcast_to(table[:, begin : begin + size], (size, size))
        down = lax.broadcasted_iota(jnp.int32, (size, size), 0)
        across = lax.broadcasted_iota(jnp.int32, (size, size), 1)
        column = jnp.sum(jnp.where(down == across, part, 0.0), axis=1, keepdims=True)
        entry = begin + lax.broadcasted_iota(jnp.int32, (size, positions.shape[1]), 0)
        found += jnp.sum(jnp.where(entry == positions, column, 0.0), axis=0, keepdims=True)
    return found


def energy_kernel(pair_index, occ_energy, vir_energy, occ_lower, occ_upper, vir_sum):
    half = occ_lower.shape[1]
    for out, begin in ((occ_lower, 0), (occ_upper, half)):
        first, second = split_index(pair_index[:, pl.ds(begin, half)], NOCC)
        out[...] = lookup(occ_energy[...], first) + lookup(occ_energy[...], second)
    width = vir_sum.shape[1]
    unordered = lax.axis_index("col") * (width // 2) + lax.broadcasted_iota(jnp.int32, (1, width), 1) // 2
    first, second = split_index(unordered, NV)
    vir_sum[...] = lookup(vir_energy[...], first) + lookup(vir_energy[...], second)


def across_rows(value):
    count = lax.axis_size("row")
    return lax.ppermute(value, "row", [(i, i ^ (count // 2)) for i in range(count)])


def across_pair(value):
    return lax.ppermute(value, "col", [(i, i ^ 1) for i in range(lax.axis_size("col"))])


def two_along(value):
    count = lax.axis_size("col")
    return lax.ppermute(value, "col", [(i, (i + 2) % count) for i in range(count)])


def shards(amplitudes, integrals, pair_index, partner, occ_energy, vir_energy):
    rows, width = amplitudes.shape
    half = rows // 2
    chunks = [half * share // sum(SHARES) for share in SHARES]
    begins = [sum(chunks[:index]) for index in range(len(chunks))]
    whole_shape = jax.ShapeDtypeStruct((rows, width), jnp.bfloat16)

    def chunk_shape(index):
        return jax.ShapeDtypeStruct((chunks[index], width), jnp.bfloat16)

    def coded_shape(index):
        return jax.ShapeDtypeStruct((chunks[index] + SCALE_ROWS, width), jnp.int16)

    half_shape = jax.ShapeDtypeStruct((1, half), jnp.float32)
    energy_shapes = [half_shape, half_shape, jax.ShapeDtypeStruct((1, width), jnp.float32)]

    own, other, moved, crossed, arrived, done, placed = {}, {}, {}, {}, {}, {}, ()
    operands = [pltpu.with_memory_space_constraint(value, pltpu.HBM) for value in (partner[None, :], amplitudes)]
    room = (pltpu.VMEM((rows, width), jnp.bfloat16), pltpu.VMEM((1, rows), jnp.int32))
    room += (pltpu.SemaphoreType.DMA((rows // chunks[0] + 1,)),)
    result = call(align_first_kernel, chunk_shape(0), operands, in_spec=HBM, scratch=room)
    other[0] = across_rows(result)
    last = (result,)
    for step, index in ORDER:
        if step == "align":
            wanted = tuple((begins[chunk], send) for chunk, send in ALIGNED[index])
            shapes = [chunk_shape(chunk) for chunk, _ in ALIGNED[index]]
            result = call(functools.partial(align_kernel, wanted), shapes, (partner[None, :], amplitudes), last)
            for (chunk, send), picked in zip(ALIGNED[index], result):
                if send:
                    other[chunk] = across_rows(picked)
                else:
                    own[chunk] = picked
            last = result[:1]
            continue
        if step == "factor":
            shapes = [jax.ShapeDtypeStruct((2 * width, width), jnp.bfloat16)] * 4
            factors = call(factor_kernel, shapes, (integrals,), last)
            last = factors[:1]
            continue
        if step == "energy":
            occ_lower, occ_upper, vir_sum = call(
                energy_kernel,
                energy_shapes,
                (pair_index[None, :], occ_energy[None, :], vir_energy[None, :]),
                last,
            )
            occ_there = across_rows(occ_upper)
            last = (vir_sum,)
            continue
        inputs = (own[index], other[index])
        if step == "first":
            result = call(first_kernel, coded_shape(index), (*inputs, factors[3]), last)
            moved[index] = two_along(result)
        elif step == "second":
            result = call(second_kernel, coded_shape(index), (*inputs, factors[1], moved[index]), last)
            crossed[index] = across_pair(result)
        elif step == "third":
            result = call(third_kernel, coded_shape(index), (*inputs, factors[2], crossed[index]), last)
            arrived[index] = two_along(result)
        elif step == "last":
            sums = (crossed[index], arrived[index], occ_lower, occ_there, vir_sum)
            result = call(functools.partial(last_kernel, begins[index]), chunk_shape(index), (*inputs, factors[0], *sums), last)
            done[index] = (result, across_rows(result))
        else:
            ready = (partner[None, :], *done[index], *placed)
            result = call(functools.partial(place_kernel, begins[index]), whole_shape, ready, last)
            placed = (result,)
        last = (result,)

    index = len(SHARES) - 1
    mine, theirs = done[index]
    picks_shape = jax.ShapeDtypeStruct((rows, chunks[index]), jnp.bfloat16)
    kernel = functools.partial(place_own_kernel, begins[index])
    most, picks = call(kernel, [whole_shape, picks_shape], (partner[None, :], mine, *placed), last)
    held = pltpu.VMEM((rows, width), jnp.bfloat16)
    arrivals = pltpu.SemaphoreType.DMA((rows // chunks[index],))
    kernel = functools.partial(place_other_kernel, begins[index])
    return call(kernel, whole_shape, (most, picks, theirs), out_spec=ANY, scratch=(held, arrivals))


def solution(mesh):
    in_specs = (P("row", "col"), P("col", None), P("row"), P("row"), P(), P())
    out_specs = P("row", "col")
    return jax.shard_map(shards, mesh=mesh, in_specs=in_specs, out_specs=out_specs, check_vma=False)
```

```python
import functools

import jax
import jax.numpy as jnp
from jax import lax
from jax.experimental import pallas as pl
from jax.experimental.pallas import tpu as pltpu
from jax.sharding import PartitionSpec as P

NOCC = 200
NV = 2000
SHARES = (2, 2, 2, 2)
SCALE_ROWS = 16
TOP = 32767.0
STEPS = 64.0
TINY = 1e-33
LANES = 128
PLACE_ROWS = 256
VMEM_LIMIT = 16 * 1024 * 1024
KERNEL_FLOPS = 4 * 10**9
ORDER = (
    (("align", 1), ("factor", 0), ("energy", 0), ("first", 0), ("align", 2), ("first", 1))
    + (("align", 3), ("first", 2), ("second", 0), ("second", 1), ("first", 3), ("third", 0))
    + (("second", 2), ("second", 3), ("third", 1), ("third", 2), ("last", 0), ("third", 3))
    + (("last", 1), ("last", 2), ("last", 3), ("place", 0), ("place", 1), ("place", 2))
)
ALIGNED = (
    (),
    ((1, True), (0, False)),
    ((2, True), (1, False)),
    ((3, True), (2, False), (3, False)),
)

VMEM = pl.BlockSpec(memory_space=pltpu.VMEM)
HBM = pl.BlockSpec(memory_space=pltpu.HBM)
ANY = pl.BlockSpec(memory_space=pl.ANY)


def call(body, out_shape, operands, after=(), in_spec=None, out_spec=None, scratch=()):
    count = len(operands)

    def kernel(*refs):
        body(*refs[:count], *refs[count + len(after) :])

    return pl.pallas_call(
        kernel,
        out_shape=out_shape,
        in_specs=[in_spec or VMEM] * count + [ANY] * len(after),
        out_specs=jax.tree.map(lambda _: out_spec or VMEM, out_shape),
        scratch_shapes=list(scratch),
        compiler_params=pltpu.CompilerParams(vmem_limit_bytes=VMEM_LIMIT),
        cost_estimate=pl.CostEstimate(flops=KERNEL_FLOPS, bytes_accessed=1, transcendentals=0),
    )(*operands, *after)


def upper_side():
    return lax.axis_index("row") // (lax.axis_size("row") // 2)


def partner_base(rows):
    return (lax.axis_index("row") ^ (lax.axis_size("row") // 2)) * rows


def exchanged(values):
    even = lax.broadcasted_iota(jnp.int32, (values.shape[0], LANES), 1) % 2 == 0
    parts = []
    for lane in range(0, values.shape[1], LANES):
        part = values[:, lane : lane + LANES]
        parts.append(jnp.where(even, pltpu.roll(part, LANES - 1, 1), pltpu.roll(part, 1, 1)))
    return jnp.concatenate(parts, axis=1)


def align_kernel(wanted, partner, amplitudes, *outs):
    rows = amplitudes.shape[0]
    upper = upper_side()

    def first(index):
        begin, send = wanted[index]
        return (1 - upper if send else upper) * (rows // 2) + begin

    @pl.when(upper == 0)
    def _():
        for index, out in enumerate(outs):
            out[...] = amplitudes[pl.ds(pl.multiple_of(first(index), LANES), out.shape[0]), :]

    @pl.when(upper == 1)
    def _():
        for index, out in enumerate(outs):
            target = partner_base(rows) + first(index) + lax.broadcasted_iota(jnp.int32, (out.shape[0], rows), 0)
            pick = jnp.where(partner[...] == target, 1.0, 0.0).astype(jnp.bfloat16)
            out[...] = jnp.dot(pick, amplitudes[...], preferred_element_type=jnp.float32).astype(jnp.bfloat16)


def align_first_kernel(partner, amplitudes, out, held, slots, arrivals):
    rows, chunk = amplitudes.shape[0], out.shape[0]
    upper = upper_side()
    first = (1 - upper) * (rows // 2)
    blocks = rows // chunk

    def fetch(block):
        part = pl.ds(block * chunk, chunk)
        return pltpu.make_async_copy(amplitudes.at[part, :], held.at[part, :], arrivals.at[block])

    @pl.when(upper == 0)
    def _():
        part = pl.ds(pl.multiple_of(first, LANES), chunk)
        straight = pltpu.make_async_copy(amplitudes.at[part, :], out, arrivals.at[0])
        straight.start()
        straight.wait()

    @pl.when(upper == 1)
    def _():
        slots_copy = pltpu.make_async_copy(partner, slots, arrivals.at[blocks])
        slots_copy.start()
        for block in range(blocks):
            fetch(block).start()
        slots_copy.wait()
        target = partner_base(rows) + first + lax.broadcasted_iota(jnp.int32, (chunk, chunk), 0)
        total = jnp.zeros(out.shape, jnp.float32)
        for block in range(blocks):
            part = pl.ds(block * chunk, chunk)
            pick = jnp.where(slots[:, part] == target, 1.0, 0.0).astype(jnp.bfloat16)
            fetch(block).wait()
            total += jnp.dot(pick, held[part, :], preferred_element_type=jnp.float32)
        out[...] = total.astype(jnp.bfloat16)


def factor_kernel(integrals, *outs):
    width = integrals.shape[0]
    for stop, out in enumerate(outs):
        block = integrals[:, pl.ds(stop * width, width)]
        out[pl.ds(0, width), :] = block
        out[pl.ds(width, width), :] = exchanged(block.astype(jnp.float32)).astype(jnp.bfloat16)


def product(own, other, factor):
    both = jnp.concatenate([own[...], other[...]], axis=1)
    return jnp.dot(both, factor[...], preferred_element_type=jnp.float32)


def code(values, out):
    rows, width = values.shape
    top = jnp.max(jnp.abs(values), axis=0, keepdims=True)
    level = jnp.ceil(STEPS * jnp.log2(jnp.maximum(top, TINY) * (1.0001 / TOP)))
    coded = jnp.round(values * jnp.exp2(level * (-1.0 / STEPS))).astype(jnp.int32).astype(jnp.int16)
    level = level.astype(jnp.int32)
    down = lax.broadcasted_iota(jnp.int32, (SCALE_ROWS, LANES), 0)
    levels = jnp.zeros((SCALE_ROWS, LANES), jnp.int32)
    for tile in range(width // LANES):
        cols = slice(tile * LANES, (tile + 1) * LANES)
        out[pl.ds(tile * rows, rows), :] = coded[:, cols]
        levels = jnp.where(down == tile, level[:, cols], levels)
    out[pl.ds(rows * width // LANES, SCALE_ROWS), :] = levels.astype(jnp.int16)


def decode(coded, rows):
    tiles = (coded.shape[0] - SCALE_ROWS) // rows
    level = coded[pl.ds(tiles * rows, SCALE_ROWS), :].astype(jnp.int32).astype(jnp.float32)
    scale = jnp.exp2(level * (1.0 / STEPS))
    parts = []
    for tile in range(tiles):
        part = coded[pl.ds(tile * rows, rows), :].astype(jnp.int32).astype(jnp.float32)
        parts.append(part * scale[tile : tile + 1, :])
    return jnp.concatenate(parts, axis=1)


def first_kernel(own, other, factor, out):
    code(product(own, other, factor), out)


def second_kernel(own, other, factor, arrived, out):
    code(product(own, other, factor) + decode(arrived, own.shape[0]), out)


def third_kernel(own, other, factor, crossed, out):
    here = jnp.where(lax.axis_index("col") % 2 == 0, 1.0, 0.0)
    code(product(own, other, factor) + decode(crossed, own.shape[0]) * here, out)


def last_kernel(begin, own, other, factor, crossed, arrived, occ_here, occ_there, vir_sum, out):
    chunk, width = out.shape
    here = jnp.where(lax.axis_index("col") % 2 == 1, 1.0, 0.0)
    total = product(own, other, factor) + decode(arrived, own.shape[0]) + decode(crossed, own.shape[0]) * here
    part = pl.ds(begin, chunk)
    occ_rows = jnp.where(upper_side() == 0, occ_here[:, part], occ_there[:, part])
    occ_down = jnp.broadcast_to(occ_rows, (LANES, chunk)).T
    for lane in range(0, width, LANES):
        denom = vir_sum[:, lane : lane + LANES] - occ_down
        out[:, lane : lane + LANES] = (total[:, lane : lane + LANES] / denom).astype(jnp.bfloat16)


def pick_rows(partner, block, size, begin, count):
    slots = jnp.broadcast_to(partner[:, pl.ds(block * size, size)], (LANES, size)).T
    lanes = lax.broadcasted_iota(jnp.int32, (size, LANES), 1) + (partner_base(partner.shape[1]) + begin)
    parts = [jnp.where(slots == lanes + lane, 1.0, 0.0) for lane in range(0, count, LANES)]
    return jnp.concatenate(parts, axis=1).astype(jnp.bfloat16)


def place_kernel(begin, partner, own, other, *refs):
    earlier, out = refs[:-1], refs[-1]
    rows, chunk = out.shape[0], own.shape[0]
    upper = upper_side()
    here = upper * (rows // 2) + begin
    there = (1 - upper) * (rows // 2) + begin
    opposite = exchanged(other[...].astype(jnp.float32)).astype(jnp.bfloat16)

    @pl.when(upper == 0)
    def _():
        if earlier:
            out[...] = earlier[0][...]
        out[pl.ds(pl.multiple_of(here, LANES), chunk), :] = own[...]
        out[pl.ds(pl.multiple_of(there, LANES), chunk), :] = opposite

    @pl.when(upper == 1)
    def _():
        for block in range(rows // PLACE_ROWS):
            part = pl.ds(block * PLACE_ROWS, PLACE_ROWS)
            pick = pick_rows(partner, block, PLACE_ROWS, here, chunk)
            found = jnp.dot(pick, own[...], preferred_element_type=jnp.float32)
            pick = pick_rows(partner, block, PLACE_ROWS, there, chunk)
            found += jnp.dot(pick, opposite, preferred_element_type=jnp.float32)
            if earlier:
                found += earlier[0][part, :].astype(jnp.float32)
            out[part, :] = found.astype(jnp.bfloat16)


def place_own_kernel(begin, partner, own, earlier, out, picks):
    rows, chunk = out.shape[0], own.shape[0]
    upper = upper_side()
    here = upper * (rows // 2) + begin
    there = (1 - upper) * (rows // 2) + begin

    @pl.when(upper == 0)
    def _():
        out[...] = earlier[...]
        out[pl.ds(pl.multiple_of(here, LANES), chunk), :] = own[...]

    @pl.when(upper == 1)
    def _():
        for block in range(rows // PLACE_ROWS):
            part = pl.ds(block * PLACE_ROWS, PLACE_ROWS)
            pick = pick_rows(partner, block, PLACE_ROWS, here, chunk)
            found = jnp.dot(pick, own[...], preferred_element_type=jnp.float32)
            out[part, :] = (found + earlier[part, :].astype(jnp.float32)).astype(jnp.bfloat16)
            picks[part, :] = pick_rows(partner, block, PLACE_ROWS, there, chunk)


def place_other_kernel(begin, earlier, picks, other, out, held, arrivals):
    rows, chunk = held.shape[0], other.shape[0]
    upper = upper_side()
    there = (1 - upper) * (rows // 2) + begin
    opposite = exchanged(other[...].astype(jnp.float32)).astype(jnp.bfloat16)

    def leave(block):
        part = pl.ds(block * chunk, chunk)
        return pltpu.make_async_copy(held.at[part, :], out.at[part, :], arrivals.at[block])

    @pl.when(upper == 0)
    def _():
        for block in range(rows // chunk):
            part = pl.ds(block * chunk, chunk)
            held[part, :] = jnp.where(there == block * chunk, opposite, earlier[part, :])
            leave(block).start()

    @pl.when(upper == 1)
    def _():
        for block in range(rows // chunk):
            part = pl.ds(block * chunk, chunk)
            found = jnp.dot(picks[part, :], opposite, preferred_element_type=jnp.float32)
            held[part, :] = (found + earlier[part, :].astype(jnp.float32)).astype(jnp.bfloat16)
            leave(block).start()

    for block in range(rows // chunk):
        leave(block).wait()


def split_index(values, count):
    high = jnp.floor((values.astype(jnp.float32) + 0.5) * (1.0 / count)).astype(jnp.int32)
    return high, values - high * count


def lookup(table, positions):
    found = jnp.zeros(positions.shape, jnp.float32)
    for begin in range(0, table.shape[1], LANES):
        size = min(LANES, table.shape[1] - begin)
        part = jnp.broadcast_to(table[:, begin : begin + size], (size, size))
        down = lax.broadcasted_iota(jnp.int32, (size, size), 0)
        across = lax.broadcasted_iota(jnp.int32, (size, size), 1)
        column = jnp.sum(jnp.where(down == across, part, 0.0), axis=1, keepdims=True)
        entry = begin + lax.broadcasted_iota(jnp.int32, (size, positions.shape[1]), 0)
        found += jnp.sum(jnp.where(entry == positions, column, 0.0), axis=0, keepdims=True)
    return found


def energy_kernel(pair_index, occ_energy, vir_energy, occ_lower, occ_upper, vir_sum):
    half = occ_lower.shape[1]
    for out, begin in ((occ_lower, 0), (occ_upper, half)):
        first, second = split_index(pair_index[:, pl.ds(begin, half)], NOCC)
        out[...] = lookup(occ_energy[...], first) + lookup(occ_energy[...], second)
    width = vir_sum.shape[1]
    unordered = lax.axis_index("col") * (width // 2) + lax.broadcasted_iota(jnp.int32, (1, width), 1) // 2
    first, second = split_index(unordered, NV)
    vir_sum[...] = lookup(vir_energy[...], first) + lookup(vir_energy[...], second)


def across_rows(value):
    count = lax.axis_size("row")
    return lax.ppermute(value, "row", [(i, i ^ (count // 2)) for i in range(count)])


def across_pair(value):
    return lax.ppermute(value, "col", [(i, i ^ 1) for i in range(lax.axis_size("col"))])


def two_along(value):
    count = lax.axis_size("col")
    return lax.ppermute(value, "col", [(i, (i + 2) % count) for i in range(count)])


def shards(amplitudes, integrals, pair_index, partner, occ_energy, vir_energy):
    rows, width = amplitudes.shape
    half = rows // 2
    chunks = [half * share // sum(SHARES) for share in SHARES]
    begins = [sum(chunks[:index]) for index in range(len(chunks))]
    whole_shape = jax.ShapeDtypeStruct((rows, width), jnp.bfloat16)

    def chunk_shape(index):
        return jax.ShapeDtypeStruct((chunks[index], width), jnp.bfloat16)

    def coded_shape(index):
        return jax.ShapeDtypeStruct((chunks[index] * (width // LANES) + SCALE_ROWS, LANES), jnp.int16)

    half_shape = jax.ShapeDtypeStruct((1, half), jnp.float32)
    energy_shapes = [half_shape, half_shape, jax.ShapeDtypeStruct((1, width), jnp.float32)]

    own, other, moved, crossed, arrived, done, placed = {}, {}, {}, {}, {}, {}, ()
    operands = [pltpu.with_memory_space_constraint(value, pltpu.HBM) for value in (partner[None, :], amplitudes)]
    room = (pltpu.VMEM((rows, width), jnp.bfloat16), pltpu.VMEM((1, rows), jnp.int32))
    room += (pltpu.SemaphoreType.DMA((rows // chunks[0] + 1,)),)
    result = call(align_first_kernel, chunk_shape(0), operands, in_spec=HBM, scratch=room)
    other[0] = across_rows(result)
    last = (result,)
    for step, index in ORDER:
        if step == "align":
            wanted = tuple((begins[chunk], send) for chunk, send in ALIGNED[index])
            shapes = [chunk_shape(chunk) for chunk, _ in ALIGNED[index]]
            result = call(functools.partial(align_kernel, wanted), shapes, (partner[None, :], amplitudes), last)
            for (chunk, send), picked in zip(ALIGNED[index], result):
                if send:
                    other[chunk] = across_rows(picked)
                else:
                    own[chunk] = picked
            last = result[:1]
            continue
        if step == "factor":
            shapes = [jax.ShapeDtypeStruct((2 * width, width), jnp.bfloat16)] * 4
            factors = call(factor_kernel, shapes, (integrals,), last)
            last = factors[:1]
            continue
        if step == "energy":
            occ_lower, occ_upper, vir_sum = call(
                energy_kernel,
                energy_shapes,
                (pair_index[None, :], occ_energy[None, :], vir_energy[None, :]),
                last,
            )
            occ_there = across_rows(occ_upper)
            last = (vir_sum,)
            continue
        inputs = (own[index], other[index])
        if step == "first":
            result = call(first_kernel, coded_shape(index), (*inputs, factors[3]), last)
            moved[index] = two_along(result)
        elif step == "second":
            result = call(second_kernel, coded_shape(index), (*inputs, factors[1], moved[index]), last)
            crossed[index] = across_pair(result)
        elif step == "third":
            result = call(third_kernel, coded_shape(index), (*inputs, factors[2], crossed[index]), last)
            arrived[index] = two_along(result)
        elif step == "last":
            sums = (crossed[index], arrived[index], occ_lower, occ_there, vir_sum)
            result = call(functools.partial(last_kernel, begins[index]), chunk_shape(index), (*inputs, factors[0], *sums), last)
            done[index] = (result, across_rows(result))
        else:
            ready = (partner[None, :], *done[index], *placed)
            result = call(functools.partial(place_kernel, begins[index]), whole_shape, ready, last)
            placed = (result,)
        last = (result,)

    index = len(SHARES) - 1
    mine, theirs = done[index]
    picks_shape = jax.ShapeDtypeStruct((rows, chunks[index]), jnp.bfloat16)
    kernel = functools.partial(place_own_kernel, begins[index])
    most, picks = call(kernel, [whole_shape, picks_shape], (partner[None, :], mine, *placed), last)
    held = pltpu.VMEM((rows, width), jnp.bfloat16)
    arrivals = pltpu.SemaphoreType.DMA((rows // chunks[index],))
    kernel = functools.partial(place_other_kernel, begins[index])
    return call(kernel, whole_shape, (most, picks, theirs), out_spec=ANY, scratch=(held, arrivals))


def solution(mesh):
    in_specs = (P("row", "col"), P("col", None), P("row"), P("row"), P(), P())
    out_specs = P("row", "col")
    return jax.shard_map(shards, mesh=mesh, in_specs=in_specs, out_specs=out_specs, check_vma=False)
```

```python
import functools

import jax
import jax.numpy as jnp
from jax import lax
from jax.experimental import pallas as pl
from jax.experimental.pallas import tpu as pltpu
from jax.sharding import PartitionSpec as P

NOCC = 200
NV = 2000
SHARES = (2, 2, 2, 2)
SCALE_ROWS = 16
TOP = 32767.0
STEPS = 64.0
TINY = 1e-33
LANES = 128
PLACE_ROWS = 256
VMEM_LIMIT = 16 * 1024 * 1024
KERNEL_FLOPS = 4 * 10**9
ORDER = (
    (("align", 1), ("factor", 0), ("energy", 0), ("first", 0), ("align", 2), ("first", 1))
    + (("align", 3), ("first", 2), ("second", 0), ("second", 1), ("first", 3), ("third", 0))
    + (("second", 2), ("second", 3), ("third", 1), ("third", 2), ("last", 0), ("third", 3))
    + (("last", 1), ("last", 2), ("last", 3), ("place", 0), ("place", 1), ("place", 2))
)
ALIGNED = (
    (),
    ((1, True), (0, False)),
    ((2, True), (1, False)),
    ((3, True), (2, False), (3, False)),
)

VMEM = pl.BlockSpec(memory_space=pltpu.VMEM)
HBM = pl.BlockSpec(memory_space=pltpu.HBM)
ANY = pl.BlockSpec(memory_space=pl.ANY)


def call(body, out_shape, operands, after=(), in_spec=None, out_spec=None, scratch=()):
    count = len(operands)

    def kernel(*refs):
        body(*refs[:count], *refs[count + len(after) :])

    return pl.pallas_call(
        kernel,
        out_shape=out_shape,
        in_specs=[in_spec or VMEM] * count + [ANY] * len(after),
        out_specs=jax.tree.map(lambda _: out_spec or VMEM, out_shape),
        scratch_shapes=list(scratch),
        compiler_params=pltpu.CompilerParams(vmem_limit_bytes=VMEM_LIMIT),
        cost_estimate=pl.CostEstimate(flops=KERNEL_FLOPS, bytes_accessed=1, transcendentals=0),
    )(*operands, *after)


def upper_side():
    return lax.axis_index("row") // (lax.axis_size("row") // 2)


def partner_base(rows):
    return (lax.axis_index("row") ^ (lax.axis_size("row") // 2)) * rows


def exchanged(values):
    even = lax.broadcasted_iota(jnp.int32, (values.shape[0], LANES), 1) % 2 == 0
    parts = []
    for lane in range(0, values.shape[1], LANES):
        part = values[:, lane : lane + LANES]
        parts.append(jnp.where(even, pltpu.roll(part, LANES - 1, 1), pltpu.roll(part, 1, 1)))
    return jnp.concatenate(parts, axis=1)


def align_kernel(wanted, partner, amplitudes, *outs):
    rows = amplitudes.shape[0]
    upper = upper_side()

    def first(index):
        begin, send = wanted[index]
        return (1 - upper if send else upper) * (rows // 2) + begin

    @pl.when(upper == 0)
    def _():
        for index, out in enumerate(outs):
            out[...] = amplitudes[pl.ds(pl.multiple_of(first(index), LANES), out.shape[0]), :]

    @pl.when(upper == 1)
    def _():
        for index, out in enumerate(outs):
            target = partner_base(rows) + first(index) + lax.broadcasted_iota(jnp.int32, (out.shape[0], rows), 0)
            pick = jnp.where(partner[...] == target, 1.0, 0.0).astype(jnp.bfloat16)
            out[...] = jnp.dot(pick, amplitudes[...], preferred_element_type=jnp.float32).astype(jnp.bfloat16)


def align_first_kernel(partner, amplitudes, out, held, slots, arrivals):
    rows, chunk = amplitudes.shape[0], out.shape[0]
    upper = upper_side()
    first = (1 - upper) * (rows // 2)
    blocks = rows // chunk

    def fetch(block):
        part = pl.ds(block * chunk, chunk)
        return pltpu.make_async_copy(amplitudes.at[part, :], held.at[part, :], arrivals.at[block])

    slots_copy = pltpu.make_async_copy(partner, slots, arrivals.at[blocks])
    slots_copy.start()
    for block in range(blocks):
        fetch(block).start()
    slots_copy.wait()

    @pl.when(upper == 0)
    def _():
        for block in range(blocks):
            fetch(block).wait()
        out[...] = held[pl.ds(pl.multiple_of(first, LANES), chunk), :]

    @pl.when(upper == 1)
    def _():
        target = partner_base(rows) + first + lax.broadcasted_iota(jnp.int32, (chunk, chunk), 0)
        total = jnp.zeros(out.shape, jnp.float32)
        for block in range(blocks):
            part = pl.ds(block * chunk, chunk)
            pick = jnp.where(slots[:, part] == target, 1.0, 0.0).astype(jnp.bfloat16)
            fetch(block).wait()
            total += jnp.dot(pick, held[part, :], preferred_element_type=jnp.float32)
        out[...] = total.astype(jnp.bfloat16)


def factor_kernel(integrals, *outs):
    width = integrals.shape[0]
    for stop, out in enumerate(outs):
        block = integrals[:, pl.ds(stop * width, width)]
        out[pl.ds(0, width), :] = block
        out[pl.ds(width, width), :] = exchanged(block.astype(jnp.float32)).astype(jnp.bfloat16)


def product(own, other, factor):
    both = jnp.concatenate([own[...], other[...]], axis=1)
    return jnp.dot(both, factor[...], preferred_element_type=jnp.float32)


def code(values, out):
    rows, width = values.shape
    top = jnp.max(jnp.abs(values), axis=0, keepdims=True)
    level = jnp.ceil(STEPS * jnp.log2(jnp.maximum(top, TINY) * (1.0001 / TOP)))
    coded = jnp.round(values * jnp.exp2(level * (-1.0 / STEPS))).astype(jnp.int32).astype(jnp.int16)
    level = level.astype(jnp.int32)
    down = lax.broadcasted_iota(jnp.int32, (SCALE_ROWS, LANES), 0)
    levels = jnp.zeros((SCALE_ROWS, LANES), jnp.int32)
    for tile in range(width // LANES):
        cols = slice(tile * LANES, (tile + 1) * LANES)
        out[pl.ds(tile * rows, rows), :] = coded[:, cols]
        levels = jnp.where(down == tile, level[:, cols], levels)
    out[pl.ds(rows * width // LANES, SCALE_ROWS), :] = levels.astype(jnp.int16)


def decode(coded, rows):
    tiles = (coded.shape[0] - SCALE_ROWS) // rows
    level = coded[pl.ds(tiles * rows, SCALE_ROWS), :].astype(jnp.int32).astype(jnp.float32)
    scale = jnp.exp2(level * (1.0 / STEPS))
    parts = []
    for tile in range(tiles):
        part = coded[pl.ds(tile * rows, rows), :].astype(jnp.int32).astype(jnp.float32)
        parts.append(part * scale[tile : tile + 1, :])
    return jnp.concatenate(parts, axis=1)


def first_kernel(own, other, factor, out):
    code(product(own, other, factor), out)


def second_kernel(own, other, factor, arrived, out):
    code(product(own, other, factor) + decode(arrived, own.shape[0]), out)


def third_kernel(own, other, factor, crossed, out):
    here = jnp.where(lax.axis_index("col") % 2 == 0, 1.0, 0.0)
    code(product(own, other, factor) + decode(crossed, own.shape[0]) * here, out)


def last_kernel(begin, own, other, factor, crossed, arrived, occ_here, occ_there, vir_sum, out):
    chunk, width = out.shape
    here = jnp.where(lax.axis_index("col") % 2 == 1, 1.0, 0.0)
    total = product(own, other, factor) + decode(arrived, own.shape[0]) + decode(crossed, own.shape[0]) * here
    part = pl.ds(begin, chunk)
    occ_rows = jnp.where(upper_side() == 0, occ_here[:, part], occ_there[:, part])
    occ_down = jnp.broadcast_to(occ_rows, (LANES, chunk)).T
    for lane in range(0, width, LANES):
        denom = vir_sum[:, lane : lane + LANES] - occ_down
        out[:, lane : lane + LANES] = (total[:, lane : lane + LANES] / denom).astype(jnp.bfloat16)


def pick_rows(partner, block, size, begin, count):
    slots = jnp.broadcast_to(partner[:, pl.ds(block * size, size)], (LANES, size)).T
    lanes = lax.broadcasted_iota(jnp.int32, (size, LANES), 1) + (partner_base(partner.shape[1]) + begin)
    parts = [jnp.where(slots == lanes + lane, 1.0, 0.0) for lane in range(0, count, LANES)]
    return jnp.concatenate(parts, axis=1).astype(jnp.bfloat16)


def place_kernel(begin, partner, own, other, *refs):
    earlier, out = refs[:-1], refs[-1]
    rows, chunk = out.shape[0], own.shape[0]
    upper = upper_side()
    here = upper * (rows // 2) + begin
    there = (1 - upper) * (rows // 2) + begin
    opposite = exchanged(other[...].astype(jnp.float32)).astype(jnp.bfloat16)

    @pl.when(upper == 0)
    def _():
        if earlier:
            out[...] = earlier[0][...]
        out[pl.ds(pl.multiple_of(here, LANES), chunk), :] = own[...]
        out[pl.ds(pl.multiple_of(there, LANES), chunk), :] = opposite

    @pl.when(upper == 1)
    def _():
        for block in range(rows // PLACE_ROWS):
            part = pl.ds(block * PLACE_ROWS, PLACE_ROWS)
            pick = pick_rows(partner, block, PLACE_ROWS, here, chunk)
            found = jnp.dot(pick, own[...], preferred_element_type=jnp.float32)
            pick = pick_rows(partner, block, PLACE_ROWS, there, chunk)
            found += jnp.dot(pick, opposite, preferred_element_type=jnp.float32)
            if earlier:
                found += earlier[0][part, :].astype(jnp.float32)
            out[part, :] = found.astype(jnp.bfloat16)


def place_own_kernel(begin, partner, own, earlier, out, picks):
    rows, chunk = out.shape[0], own.shape[0]
    upper = upper_side()
    here = upper * (rows // 2) + begin
    there = (1 - upper) * (rows // 2) + begin

    @pl.when(upper == 0)
    def _():
        out[...] = earlier[...]
        out[pl.ds(pl.multiple_of(here, LANES), chunk), :] = own[...]

    @pl.when(upper == 1)
    def _():
        for block in range(rows // PLACE_ROWS):
            part = pl.ds(block * PLACE_ROWS, PLACE_ROWS)
            pick = pick_rows(partner, block, PLACE_ROWS, here, chunk)
            found = jnp.dot(pick, own[...], preferred_element_type=jnp.float32)
            out[part, :] = (found + earlier[part, :].astype(jnp.float32)).astype(jnp.bfloat16)
            picks[part, :] = pick_rows(partner, block, PLACE_ROWS, there, chunk)


def place_other_kernel(begin, earlier, picks, other, out, held, arrivals):
    rows, chunk = held.shape[0], other.shape[0]
    upper = upper_side()
    there = (1 - upper) * (rows // 2) + begin
    opposite = exchanged(other[...].astype(jnp.float32)).astype(jnp.bfloat16)

    def leave(block):
        part = pl.ds(block * chunk, chunk)
        return pltpu.make_async_copy(held.at[part, :], out.at[part, :], arrivals.at[block])

    @pl.when(upper == 0)
    def _():
        for block in range(rows // chunk):
            part = pl.ds(block * chunk, chunk)
            held[part, :] = jnp.where(there == block * chunk, opposite, earlier[part, :])
            leave(block).start()

    @pl.when(upper == 1)
    def _():
        for block in range(rows // chunk):
            part = pl.ds(block * chunk, chunk)
            found = jnp.dot(picks[part, :], opposite, preferred_element_type=jnp.float32)
            held[part, :] = (found + earlier[part, :].astype(jnp.float32)).astype(jnp.bfloat16)
            leave(block).start()

    for block in range(rows // chunk):
        leave(block).wait()


def split_index(values, count):
    high = jnp.floor((values.astype(jnp.float32) + 0.5) * (1.0 / count)).astype(jnp.int32)
    return high, values - high * count


def lookup(table, positions):
    found = jnp.zeros(positions.shape, jnp.float32)
    for begin in range(0, table.shape[1], LANES):
        size = min(LANES, table.shape[1] - begin)
        part = jnp.broadcast_to(table[:, begin : begin + size], (size, size))
        down = lax.broadcasted_iota(jnp.int32, (size, size), 0)
        across = lax.broadcasted_iota(jnp.int32, (size, size), 1)
        column = jnp.sum(jnp.where(down == across, part, 0.0), axis=1, keepdims=True)
        entry = begin + lax.broadcasted_iota(jnp.int32, (size, positions.shape[1]), 0)
        found += jnp.sum(jnp.where(entry == positions, column, 0.0), axis=0, keepdims=True)
    return found


def energy_kernel(pair_index, occ_energy, vir_energy, occ_lower, occ_upper, vir_sum):
    half = occ_lower.shape[1]
    for out, begin in ((occ_lower, 0), (occ_upper, half)):
        first, second = split_index(pair_index[:, pl.ds(begin, half)], NOCC)
        out[...] = lookup(occ_energy[...], first) + lookup(occ_energy[...], second)
    width = vir_sum.shape[1]
    unordered = lax.axis_index("col") * (width // 2) + lax.broadcasted_iota(jnp.int32, (1, width), 1) // 2
    first, second = split_index(unordered, NV)
    vir_sum[...] = lookup(vir_energy[...], first) + lookup(vir_energy[...], second)


def across_rows(value):
    count = lax.axis_size("row")
    return lax.ppermute(value, "row", [(i, i ^ (count // 2)) for i in range(count)])


def across_pair(value):
    return lax.ppermute(value, "col", [(i, i ^ 1) for i in range(lax.axis_size("col"))])


def two_along(value):
    count = lax.axis_size("col")
    return lax.ppermute(value, "col", [(i, (i + 2) % count) for i in range(count)])


def shards(amplitudes, integrals, pair_index, partner, occ_energy, vir_energy):
    rows, width = amplitudes.shape
    half = rows // 2
    chunks = [half * share // sum(SHARES) for share in SHARES]
    begins = [sum(chunks[:index]) for index in range(len(chunks))]
    whole_shape = jax.ShapeDtypeStruct((rows, width), jnp.bfloat16)

    def chunk_shape(index):
        return jax.ShapeDtypeStruct((chunks[index], width), jnp.bfloat16)

    def coded_shape(index):
        return jax.ShapeDtypeStruct((chunks[index] * (width // LANES) + SCALE_ROWS, LANES), jnp.int16)

    half_shape = jax.ShapeDtypeStruct((1, half), jnp.float32)
    energy_shapes = [half_shape, half_shape, jax.ShapeDtypeStruct((1, width), jnp.float32)]

    own, other, moved, crossed, arrived, done, placed = {}, {}, {}, {}, {}, {}, ()
    operands = [pltpu.with_memory_space_constraint(value, pltpu.HBM) for value in (partner[None, :], amplitudes)]
    room = (pltpu.VMEM((1, rows), jnp.int32), pltpu.SemaphoreType.DMA((rows // chunks[0] + 1,)))
    result, held = call(align_first_kernel, [chunk_shape(0), whole_shape], operands, in_spec=HBM, scratch=room)
    other[0] = across_rows(result)
    last = (result,)
    for step, index in ORDER:
        if step == "align":
            wanted = tuple((begins[chunk], send) for chunk, send in ALIGNED[index])
            shapes = [chunk_shape(chunk) for chunk, _ in ALIGNED[index]]
            result = call(functools.partial(align_kernel, wanted), shapes, (partner[None, :], held), last)
            for (chunk, send), picked in zip(ALIGNED[index], result):
                if send:
                    other[chunk] = across_rows(picked)
                else:
                    own[chunk] = picked
            last = result[:1]
            continue
        if step == "factor":
            shapes = [jax.ShapeDtypeStruct((2 * width, width), jnp.bfloat16)] * 4
            factors = call(factor_kernel, shapes, (integrals,), last)
            last = factors[:1]
            continue
        if step == "energy":
            occ_lower, occ_upper, vir_sum = call(
                energy_kernel,
                energy_shapes,
                (pair_index[None, :], occ_energy[None, :], vir_energy[None, :]),
                last,
            )
            occ_there = across_rows(occ_upper)
            last = (vir_sum,)
            continue
        inputs = (own[index], other[index])
        if step == "first":
            result = call(first_kernel, coded_shape(index), (*inputs, factors[3]), last)
            moved[index] = two_along(result)
        elif step == "second":
            result = call(second_kernel, coded_shape(index), (*inputs, factors[1], moved[index]), last)
            crossed[index] = across_pair(result)
        elif step == "third":
            result = call(third_kernel, coded_shape(index), (*inputs, factors[2], crossed[index]), last)
            arrived[index] = two_along(result)
        elif step == "last":
            sums = (crossed[index], arrived[index], occ_lower, occ_there, vir_sum)
            result = call(functools.partial(last_kernel, begins[index]), chunk_shape(index), (*inputs, factors[0], *sums), last)
            done[index] = (result, across_rows(result))
        else:
            ready = (partner[None, :], *done[index], *placed)
            result = call(functools.partial(place_kernel, begins[index]), whole_shape, ready, last)
            placed = (result,)
        last = (result,)

    index = len(SHARES) - 1
    mine, theirs = done[index]
    picks_shape = jax.ShapeDtypeStruct((rows, chunks[index]), jnp.bfloat16)
    kernel = functools.partial(place_own_kernel, begins[index])
    most, picks = call(kernel, [whole_shape, picks_shape], (partner[None, :], mine, *placed), last)
    room = pltpu.VMEM((rows, width), jnp.bfloat16)
    arrivals = pltpu.SemaphoreType.DMA((rows // chunks[index],))
    kernel = functools.partial(place_other_kernel, begins[index])
    return call(kernel, whole_shape, (most, picks, theirs), out_spec=ANY, scratch=(room, arrivals))


def solution(mesh):
    in_specs = (P("row", "col"), P("col", None), P("row"), P("row"), P(), P())
    out_specs = P("row", "col")
    return jax.shard_map(shards, mesh=mesh, in_specs=in_specs, out_specs=out_specs, check_vma=False)
```

```python
import functools

import jax
import jax.numpy as jnp
from jax import lax
from jax.experimental import pallas as pl
from jax.experimental.pallas import tpu as pltpu
from jax.sharding import PartitionSpec as P

NOCC = 200
NV = 2000
SHARES = (2, 2, 2, 2)
SCALE_ROWS = 16
TOP = 32767.0
STEPS = 64.0
TINY = 1e-33
LANES = 128
PLACE_ROWS = 256
VMEM_LIMIT = 16 * 1024 * 1024
KERNEL_FLOPS = 4 * 10**9
ORDER = (
    (("align", 1), ("factor", 0), ("energy", 0), ("first", 0), ("align", 2), ("first", 1))
    + (("align", 3), ("first", 2), ("second", 0), ("second", 1), ("first", 3), ("third", 0))
    + (("second", 2), ("second", 3), ("third", 1), ("third", 2), ("last", 0), ("third", 3))
    + (("last", 1), ("last", 2), ("last", 3), ("place", 0), ("place", 1), ("place", 2))
)
ALIGNED = (
    (),
    ((1, True), (0, False)),
    ((2, True), (1, False)),
    ((3, True), (2, False), (3, False)),
)

VMEM = pl.BlockSpec(memory_space=pltpu.VMEM)
HBM = pl.BlockSpec(memory_space=pltpu.HBM)
ANY = pl.BlockSpec(memory_space=pl.ANY)


def call(body, out_shape, operands, after=(), in_spec=None, out_spec=None, scratch=()):
    count = len(operands)

    def kernel(*refs):
        body(*refs[:count], *refs[count + len(after) :])

    return pl.pallas_call(
        kernel,
        out_shape=out_shape,
        in_specs=[in_spec or VMEM] * count + [ANY] * len(after),
        out_specs=jax.tree.map(lambda _: out_spec or VMEM, out_shape),
        scratch_shapes=list(scratch),
        compiler_params=pltpu.CompilerParams(vmem_limit_bytes=VMEM_LIMIT),
        cost_estimate=pl.CostEstimate(flops=KERNEL_FLOPS, bytes_accessed=1, transcendentals=0),
    )(*operands, *after)


def upper_side():
    return lax.axis_index("row") // (lax.axis_size("row") // 2)


def partner_base(rows):
    return (lax.axis_index("row") ^ (lax.axis_size("row") // 2)) * rows


def exchanged(values):
    even = lax.broadcasted_iota(jnp.int32, (values.shape[0], LANES), 1) % 2 == 0
    parts = []
    for lane in range(0, values.shape[1], LANES):
        part = values[:, lane : lane + LANES]
        parts.append(jnp.where(even, pltpu.roll(part, LANES - 1, 1), pltpu.roll(part, 1, 1)))
    return jnp.concatenate(parts, axis=1)


def align_kernel(wanted, partner, amplitudes, *outs):
    rows = amplitudes.shape[0]
    upper = upper_side()

    def first(index):
        begin, send = wanted[index]
        return (1 - upper if send else upper) * (rows // 2) + begin

    @pl.when(upper == 0)
    def _():
        for index, out in enumerate(outs):
            out[...] = amplitudes[pl.ds(pl.multiple_of(first(index), LANES), out.shape[0]), :]

    @pl.when(upper == 1)
    def _():
        for index, out in enumerate(outs):
            target = partner_base(rows) + first(index) + lax.broadcasted_iota(jnp.int32, (out.shape[0], rows), 0)
            pick = jnp.where(partner[...] == target, 1.0, 0.0).astype(jnp.bfloat16)
            out[...] = jnp.dot(pick, amplitudes[...], preferred_element_type=jnp.float32).astype(jnp.bfloat16)


def align_first_kernel(partner, amplitudes, out, held, slots, arrivals):
    rows, chunk = amplitudes.shape[0], out.shape[0]
    upper = upper_side()
    first = (1 - upper) * (rows // 2)
    blocks = rows // chunk

    def fetch(block):
        part = pl.ds(block * chunk, chunk)
        return pltpu.make_async_copy(amplitudes.at[part, :], held.at[part, :], arrivals.at[block])

    slots_copy = pltpu.make_async_copy(partner, slots, arrivals.at[blocks])
    slots_copy.start()
    for block in range(blocks):
        fetch(block).start()
    slots_copy.wait()

    @pl.when(upper == 0)
    def _():
        for block in range(blocks):
            fetch(block).wait()
        out[...] = held[pl.ds(pl.multiple_of(first, LANES), chunk), :]

    @pl.when(upper == 1)
    def _():
        target = partner_base(rows) + first + lax.broadcasted_iota(jnp.int32, (chunk, chunk), 0)
        total = jnp.zeros(out.shape, jnp.float32)
        for block in range(blocks):
            part = pl.ds(block * chunk, chunk)
            pick = jnp.where(slots[:, part] == target, 1.0, 0.0).astype(jnp.bfloat16)
            fetch(block).wait()
            total += jnp.dot(pick, held[part, :], preferred_element_type=jnp.float32)
        out[...] = total.astype(jnp.bfloat16)


def factor_kernel(integrals, *outs):
    width = integrals.shape[0]
    for stop, out in enumerate(outs):
        block = integrals[:, pl.ds(stop * width, width)]
        out[pl.ds(0, width), :] = block
        out[pl.ds(width, width), :] = exchanged(block.astype(jnp.float32)).astype(jnp.bfloat16)


def product(own, other, factor):
    both = jnp.concatenate([own[...], other[...]], axis=1)
    return jnp.dot(both, factor[...], preferred_element_type=jnp.float32)


def code(values, out):
    rows, width = values.shape
    top = jnp.max(jnp.abs(values), axis=0, keepdims=True)
    level = jnp.ceil(STEPS * jnp.log2(jnp.maximum(top, TINY) * (1.0001 / TOP)))
    coded = jnp.round(values * jnp.exp2(level * (-1.0 / STEPS))).astype(jnp.int32).astype(jnp.int16)
    level = level.astype(jnp.int32)
    down = lax.broadcasted_iota(jnp.int32, (SCALE_ROWS, LANES), 0)
    levels = jnp.zeros((SCALE_ROWS, LANES), jnp.int32)
    for tile in range(width // LANES):
        cols = slice(tile * LANES, (tile + 1) * LANES)
        out[pl.ds(tile * rows, rows), :] = coded[:, cols]
        levels = jnp.where(down == tile, level[:, cols], levels)
    out[pl.ds(rows * width // LANES, SCALE_ROWS), :] = levels.astype(jnp.int16)


def decode(coded, rows):
    tiles = (coded.shape[0] - SCALE_ROWS) // rows
    level = coded[pl.ds(tiles * rows, SCALE_ROWS), :].astype(jnp.int32).astype(jnp.float32)
    scale = jnp.exp2(level * (1.0 / STEPS))
    parts = []
    for tile in range(tiles):
        part = coded[pl.ds(tile * rows, rows), :].astype(jnp.int32).astype(jnp.float32)
        parts.append(part * scale[tile : tile + 1, :])
    return jnp.concatenate(parts, axis=1)


def first_kernel(own, other, factor, out):
    code(product(own, other, factor), out)


def second_kernel(own, other, factor, arrived, out):
    code(product(own, other, factor) + decode(arrived, own.shape[0]), out)


def third_kernel(own, other, factor, crossed, out):
    here = jnp.where(lax.axis_index("col") % 2 == 0, 1.0, 0.0)
    code(product(own, other, factor) + decode(crossed, own.shape[0]) * here, out)


def last_kernel(begin, own, other, factor, crossed, arrived, occ_here, occ_there, vir_sum, out):
    chunk, width = out.shape
    here = jnp.where(lax.axis_index("col") % 2 == 1, 1.0, 0.0)
    total = product(own, other, factor) + decode(arrived, own.shape[0]) + decode(crossed, own.shape[0]) * here
    part = pl.ds(begin, chunk)
    occ_rows = jnp.where(upper_side() == 0, occ_here[:, part], occ_there[:, part])
    occ_down = jnp.broadcast_to(occ_rows, (LANES, chunk)).T
    for lane in range(0, width, LANES):
        denom = vir_sum[:, lane : lane + LANES] - occ_down
        out[:, lane : lane + LANES] = (total[:, lane : lane + LANES] / denom).astype(jnp.bfloat16)


def pick_rows(partner, block, size, begin, count):
    slots = jnp.broadcast_to(partner[:, pl.ds(block * size, size)], (LANES, size)).T
    lanes = lax.broadcasted_iota(jnp.int32, (size, LANES), 1) + (partner_base(partner.shape[1]) + begin)
    parts = [jnp.where(slots == lanes + lane, 1.0, 0.0) for lane in range(0, count, LANES)]
    return jnp.concatenate(parts, axis=1).astype(jnp.bfloat16)


def place_kernel(begin, partner, own, other, *refs):
    earlier, out = refs[:-1], refs[-1]
    rows, chunk = out.shape[0], own.shape[0]
    upper = upper_side()
    here = upper * (rows // 2) + begin
    there = (1 - upper) * (rows // 2) + begin
    opposite = exchanged(other[...].astype(jnp.float32)).astype(jnp.bfloat16)

    @pl.when(upper == 0)
    def _():
        if earlier:
            out[...] = earlier[0][...]
        out[pl.ds(pl.multiple_of(here, LANES), chunk), :] = own[...]
        out[pl.ds(pl.multiple_of(there, LANES), chunk), :] = opposite

    @pl.when(upper == 1)
    def _():
        for block in range(rows // PLACE_ROWS):
            part = pl.ds(block * PLACE_ROWS, PLACE_ROWS)
            pick = pick_rows(partner, block, PLACE_ROWS, here, chunk)
            found = jnp.dot(pick, own[...], preferred_element_type=jnp.float32)
            pick = pick_rows(partner, block, PLACE_ROWS, there, chunk)
            found += jnp.dot(pick, opposite, preferred_element_type=jnp.float32)
            if earlier:
                found += earlier[0][part, :].astype(jnp.float32)
            out[part, :] = found.astype(jnp.bfloat16)


def place_own_kernel(begin, partner, own, earlier, out, picks):
    rows, chunk = out.shape[0], own.shape[0]
    upper = upper_side()
    here = upper * (rows // 2) + begin
    there = (1 - upper) * (rows // 2) + begin

    @pl.when(upper == 0)
    def _():
        out[...] = earlier[...]
        out[pl.ds(pl.multiple_of(here, LANES), chunk), :] = own[...]

    @pl.when(upper == 1)
    def _():
        for block in range(rows // PLACE_ROWS):
            part = pl.ds(block * PLACE_ROWS, PLACE_ROWS)
            pick = pick_rows(partner, block, PLACE_ROWS, here, chunk)
            found = jnp.dot(pick, own[...], preferred_element_type=jnp.float32)
            out[part, :] = (found + earlier[part, :].astype(jnp.float32)).astype(jnp.bfloat16)
            picks[part, :] = pick_rows(partner, block, PLACE_ROWS, there, chunk)


def place_other_kernel(begin, earlier, picks, other, out, held, arrivals):
    rows, chunk = held.shape[0], other.shape[0]
    upper = upper_side()
    there = (1 - upper) * (rows // 2) + begin
    size = chunk // 2

    def leave(block):
        part = pl.ds(block * size, size)
        return pltpu.make_async_copy(held.at[part, :], out.at[part, :], arrivals.at[block])

    opposite = exchanged(other[...].astype(jnp.float32)).astype(jnp.bfloat16)

    @pl.when(upper == 0)
    def _():
        for block in range(rows // size):
            part = pl.ds(block * size, size)
            half = opposite[size * (block % 2) : size * (block % 2 + 1), :]
            held[part, :] = jnp.where(there == block // 2 * chunk, half, earlier[part, :])
            leave(block).start()

    @pl.when(upper == 1)
    def _():
        for block in range(rows // size):
            part = pl.ds(block * size, size)
            found = jnp.dot(picks[part, :], opposite, preferred_element_type=jnp.float32)
            held[part, :] = (found + earlier[part, :].astype(jnp.float32)).astype(jnp.bfloat16)
            leave(block).start()

    for block in range(rows // size):
        leave(block).wait()


def split_index(values, count):
    high = jnp.floor((values.astype(jnp.float32) + 0.5) * (1.0 / count)).astype(jnp.int32)
    return high, values - high * count


def lookup(table, positions):
    found = jnp.zeros(positions.shape, jnp.float32)
    for begin in range(0, table.shape[1], LANES):
        size = min(LANES, table.shape[1] - begin)
        part = jnp.broadcast_to(table[:, begin : begin + size], (size, size))
        down = lax.broadcasted_iota(jnp.int32, (size, size), 0)
        across = lax.broadcasted_iota(jnp.int32, (size, size), 1)
        column = jnp.sum(jnp.where(down == across, part, 0.0), axis=1, keepdims=True)
        entry = begin + lax.broadcasted_iota(jnp.int32, (size, positions.shape[1]), 0)
        found += jnp.sum(jnp.where(entry == positions, column, 0.0), axis=0, keepdims=True)
    return found


def energy_kernel(pair_index, occ_energy, vir_energy, occ_lower, occ_upper, vir_sum):
    half = occ_lower.shape[1]
    for out, begin in ((occ_lower, 0), (occ_upper, half)):
        first, second = split_index(pair_index[:, pl.ds(begin, half)], NOCC)
        out[...] = lookup(occ_energy[...], first) + lookup(occ_energy[...], second)
    width = vir_sum.shape[1]
    unordered = lax.axis_index("col") * (width // 2) + lax.broadcasted_iota(jnp.int32, (1, width), 1) // 2
    first, second = split_index(unordered, NV)
    vir_sum[...] = lookup(vir_energy[...], first) + lookup(vir_energy[...], second)


def across_rows(value):
    count = lax.axis_size("row")
    return lax.ppermute(value, "row", [(i, i ^ (count // 2)) for i in range(count)])


def across_pair(value):
    return lax.ppermute(value, "col", [(i, i ^ 1) for i in range(lax.axis_size("col"))])


def two_along(value):
    count = lax.axis_size("col")
    return lax.ppermute(value, "col", [(i, (i + 2) % count) for i in range(count)])


def shards(amplitudes, integrals, pair_index, partner, occ_energy, vir_energy):
    rows, width = amplitudes.shape
    half = rows // 2
    chunks = [half * share // sum(SHARES) for share in SHARES]
    begins = [sum(chunks[:index]) for index in range(len(chunks))]
    whole_shape = jax.ShapeDtypeStruct((rows, width), jnp.bfloat16)

    def chunk_shape(index):
        return jax.ShapeDtypeStruct((chunks[index], width), jnp.bfloat16)

    def coded_shape(index):
        return jax.ShapeDtypeStruct((chunks[index] * (width // LANES) + SCALE_ROWS, LANES), jnp.int16)

    half_shape = jax.ShapeDtypeStruct((1, half), jnp.float32)
    energy_shapes = [half_shape, half_shape, jax.ShapeDtypeStruct((1, width), jnp.float32)]

    own, other, moved, crossed, arrived, done, placed = {}, {}, {}, {}, {}, {}, ()
    operands = [pltpu.with_memory_space_constraint(value, pltpu.HBM) for value in (partner[None, :], amplitudes)]
    room = (pltpu.VMEM((1, rows), jnp.int32), pltpu.SemaphoreType.DMA((rows // chunks[0] + 1,)))
    result, held = call(align_first_kernel, [chunk_shape(0), whole_shape], operands, in_spec=HBM, scratch=room)
    other[0] = across_rows(result)
    last = (result,)
    for step, index in ORDER:
        if step == "align":
            wanted = tuple((begins[chunk], send) for chunk, send in ALIGNED[index])
            shapes = [chunk_shape(chunk) for chunk, _ in ALIGNED[index]]
            result = call(functools.partial(align_kernel, wanted), shapes, (partner[None, :], held), last)
            for (chunk, send), picked in zip(ALIGNED[index], result):
                if send:
                    other[chunk] = across_rows(picked)
                else:
                    own[chunk] = picked
            last = result[:1]
            continue
        if step == "factor":
            shapes = [jax.ShapeDtypeStruct((2 * width, width), jnp.bfloat16)] * 4
            factors = call(factor_kernel, shapes, (integrals,), last)
            last = factors[:1]
            continue
        if step == "energy":
            occ_lower, occ_upper, vir_sum = call(
                energy_kernel,
                energy_shapes,
                (pair_index[None, :], occ_energy[None, :], vir_energy[None, :]),
                last,
            )
            occ_there = across_rows(occ_upper)
            last = (vir_sum,)
            continue
        inputs = (own[index], other[index])
        if step == "first":
            result = call(first_kernel, coded_shape(index), (*inputs, factors[3]), last)
            moved[index] = two_along(result)
        elif step == "second":
            result = call(second_kernel, coded_shape(index), (*inputs, factors[1], moved[index]), last)
            crossed[index] = across_pair(result)
        elif step == "third":
            result = call(third_kernel, coded_shape(index), (*inputs, factors[2], crossed[index]), last)
            arrived[index] = two_along(result)
        elif step == "last":
            sums = (crossed[index], arrived[index], occ_lower, occ_there, vir_sum)
            result = call(functools.partial(last_kernel, begins[index]), chunk_shape(index), (*inputs, factors[0], *sums), last)
            done[index] = (result, across_rows(result))
        else:
            ready = (partner[None, :], *done[index], *placed)
            result = call(functools.partial(place_kernel, begins[index]), whole_shape, ready, last)
            placed = (result,)
        last = (result,)

    index = len(SHARES) - 1
    mine, theirs = done[index]
    picks_shape = jax.ShapeDtypeStruct((rows, chunks[index]), jnp.bfloat16)
    kernel = functools.partial(place_own_kernel, begins[index])
    most, picks = call(kernel, [whole_shape, picks_shape], (partner[None, :], mine, *placed), last)
    room = pltpu.VMEM((rows, width), jnp.bfloat16)
    arrivals = pltpu.SemaphoreType.DMA((2 * rows // chunks[index],))
    kernel = functools.partial(place_other_kernel, begins[index])
    return call(kernel, whole_shape, (most, picks, theirs), out_spec=ANY, scratch=(room, arrivals))


def solution(mesh):
    in_specs = (P("row", "col"), P("col", None), P("row"), P("row"), P(), P())
    out_specs = P("row", "col")
    return jax.shard_map(shards, mesh=mesh, in_specs=in_specs, out_specs=out_specs, check_vma=False)
```

```python
import functools

import jax
import jax.numpy as jnp
from jax import lax
from jax.experimental import pallas as pl
from jax.experimental.pallas import tpu as pltpu
from jax.sharding import PartitionSpec as P

NOCC = 200
NV = 2000
SHARES = (2, 2, 2, 2)
SCALE_ROWS = 16
TOP = 32767.0
STEPS = 64.0
TINY = 1e-33
LANES = 128
PLACE_ROWS = 256
VMEM_LIMIT = 16 * 1024 * 1024
KERNEL_FLOPS = 4 * 10**9
ORDER = (
    (("align", 1), ("factor", 0), ("energy", 0), ("first", 0), ("align", 2), ("first", 1))
    + (("align", 3), ("first", 2), ("second", 0), ("second", 1), ("first", 3), ("third", 0))
    + (("second", 2), ("second", 3), ("third", 1), ("third", 2), ("last", 0), ("third", 3))
    + (("last", 1), ("last", 2), ("place", 0), ("last", 3), ("place", 1), ("place", 2))
)
ALIGNED = (
    (),
    ((1, True), (0, False)),
    ((2, True), (1, False)),
    ((3, True), (2, False), (3, False)),
)

VMEM = pl.BlockSpec(memory_space=pltpu.VMEM)
HBM = pl.BlockSpec(memory_space=pltpu.HBM)
ANY = pl.BlockSpec(memory_space=pl.ANY)


def call(body, out_shape, operands, after=(), in_spec=None, out_spec=None, scratch=()):
    count = len(operands)

    def kernel(*refs):
        body(*refs[:count], *refs[count + len(after) :])

    return pl.pallas_call(
        kernel,
        out_shape=out_shape,
        in_specs=[in_spec or VMEM] * count + [ANY] * len(after),
        out_specs=jax.tree.map(lambda _: out_spec or VMEM, out_shape),
        scratch_shapes=list(scratch),
        compiler_params=pltpu.CompilerParams(vmem_limit_bytes=VMEM_LIMIT),
        cost_estimate=pl.CostEstimate(flops=KERNEL_FLOPS, bytes_accessed=1, transcendentals=0),
    )(*operands, *after)


def upper_side():
    return lax.axis_index("row") // (lax.axis_size("row") // 2)


def partner_base(rows):
    return (lax.axis_index("row") ^ (lax.axis_size("row") // 2)) * rows


def exchanged(values):
    even = lax.broadcasted_iota(jnp.int32, (values.shape[0], LANES), 1) % 2 == 0
    parts = []
    for lane in range(0, values.shape[1], LANES):
        part = values[:, lane : lane + LANES]
        parts.append(jnp.where(even, pltpu.roll(part, LANES - 1, 1), pltpu.roll(part, 1, 1)))
    return jnp.concatenate(parts, axis=1)


def align_kernel(wanted, partner, amplitudes, *outs):
    rows = amplitudes.shape[0]
    upper = upper_side()

    def first(index):
        begin, send = wanted[index]
        return (1 - upper if send else upper) * (rows // 2) + begin

    @pl.when(upper == 0)
    def _():
        for index, out in enumerate(outs):
            out[...] = amplitudes[pl.ds(pl.multiple_of(first(index), LANES), out.shape[0]), :]

    @pl.when(upper == 1)
    def _():
        for index, out in enumerate(outs):
            target = partner_base(rows) + first(index) + lax.broadcasted_iota(jnp.int32, (out.shape[0], rows), 0)
            pick = jnp.where(partner[...] == target, 1.0, 0.0).astype(jnp.bfloat16)
            out[...] = jnp.dot(pick, amplitudes[...], preferred_element_type=jnp.float32).astype(jnp.bfloat16)


def align_first_kernel(partner, amplitudes, out, held, slots, arrivals):
    rows, chunk = amplitudes.shape[0], out.shape[0]
    upper = upper_side()
    first = (1 - upper) * (rows // 2)
    blocks = rows // chunk

    def fetch(block):
        part = pl.ds(block * chunk, chunk)
        return pltpu.make_async_copy(amplitudes.at[part, :], held.at[part, :], arrivals.at[block])

    slots_copy = pltpu.make_async_copy(partner, slots, arrivals.at[blocks])
    slots_copy.start()
    for block in range(blocks):
        fetch(block).start()
    slots_copy.wait()

    @pl.when(upper == 0)
    def _():
        for block in range(blocks):
            fetch(block).wait()
        out[...] = held[pl.ds(pl.multiple_of(first, LANES), chunk), :]

    @pl.when(upper == 1)
    def _():
        target = partner_base(rows) + first + lax.broadcasted_iota(jnp.int32, (chunk, chunk), 0)
        total = jnp.zeros(out.shape, jnp.float32)
        for block in range(blocks):
            part = pl.ds(block * chunk, chunk)
            pick = jnp.where(slots[:, part] == target, 1.0, 0.0).astype(jnp.bfloat16)
            fetch(block).wait()
            total += jnp.dot(pick, held[part, :], preferred_element_type=jnp.float32)
        out[...] = total.astype(jnp.bfloat16)


def factor_kernel(integrals, *outs):
    width = integrals.shape[0]
    for stop, out in enumerate(outs):
        block = integrals[:, pl.ds(stop * width, width)]
        out[pl.ds(0, width), :] = block
        out[pl.ds(width, width), :] = exchanged(block.astype(jnp.float32)).astype(jnp.bfloat16)


def product(own, other, factor):
    both = jnp.concatenate([own[...], other[...]], axis=1)
    return jnp.dot(both, factor[...], preferred_element_type=jnp.float32)


def code(values, out):
    rows, width = values.shape
    top = jnp.max(jnp.abs(values), axis=0, keepdims=True)
    level = jnp.ceil(STEPS * jnp.log2(jnp.maximum(top, TINY) * (1.0001 / TOP)))
    coded = jnp.round(values * jnp.exp2(level * (-1.0 / STEPS))).astype(jnp.int32).astype(jnp.int16)
    level = level.astype(jnp.int32)
    down = lax.broadcasted_iota(jnp.int32, (SCALE_ROWS, LANES), 0)
    levels = jnp.zeros((SCALE_ROWS, LANES), jnp.int32)
    for tile in range(width // LANES):
        cols = slice(tile * LANES, (tile + 1) * LANES)
        out[pl.ds(tile * rows, rows), :] = coded[:, cols]
        levels = jnp.where(down == tile, level[:, cols], levels)
    out[pl.ds(rows * width // LANES, SCALE_ROWS), :] = levels.astype(jnp.int16)


def decode(coded, rows):
    tiles = (coded.shape[0] - SCALE_ROWS) // rows
    level = coded[pl.ds(tiles * rows, SCALE_ROWS), :].astype(jnp.int32).astype(jnp.float32)
    scale = jnp.exp2(level * (1.0 / STEPS))
    parts = []
    for tile in range(tiles):
        part = coded[pl.ds(tile * rows, rows), :].astype(jnp.int32).astype(jnp.float32)
        parts.append(part * scale[tile : tile + 1, :])
    return jnp.concatenate(parts, axis=1)


def first_kernel(own, other, factor, out):
    code(product(own, other, factor), out)


def second_kernel(own, other, factor, arrived, out):
    code(product(own, other, factor) + decode(arrived, own.shape[0]), out)


def third_kernel(own, other, factor, crossed, out):
    here = jnp.where(lax.axis_index("col") % 2 == 0, 1.0, 0.0)
    code(product(own, other, factor) + decode(crossed, own.shape[0]) * here, out)


def last_kernel(begin, own, other, factor, crossed, arrived, occ_here, occ_there, vir_sum, out):
    chunk, width = out.shape
    here = jnp.where(lax.axis_index("col") % 2 == 1, 1.0, 0.0)
    total = product(own, other, factor) + decode(arrived, own.shape[0]) + decode(crossed, own.shape[0]) * here
    part = pl.ds(begin, chunk)
    occ_rows = jnp.where(upper_side() == 0, occ_here[:, part], occ_there[:, part])
    occ_down = jnp.broadcast_to(occ_rows, (LANES, chunk)).T
    for lane in range(0, width, LANES):
        denom = vir_sum[:, lane : lane + LANES] - occ_down
        out[:, lane : lane + LANES] = (total[:, lane : lane + LANES] / denom).astype(jnp.bfloat16)


def pick_rows(partner, block, size, begin, count):
    slots = jnp.broadcast_to(partner[:, pl.ds(block * size, size)], (LANES, size)).T
    lanes = lax.broadcasted_iota(jnp.int32, (size, LANES), 1) + (partner_base(partner.shape[1]) + begin)
    parts = [jnp.where(slots == lanes + lane, 1.0, 0.0) for lane in range(0, count, LANES)]
    return jnp.concatenate(parts, axis=1).astype(jnp.bfloat16)


def place_kernel(begin, partner, own, other, *refs):
    earlier, out = refs[:-1], refs[-1]
    rows, chunk = out.shape[0], own.shape[0]
    upper = upper_side()
    here = upper * (rows // 2) + begin
    there = (1 - upper) * (rows // 2) + begin
    opposite = exchanged(other[...].astype(jnp.float32)).astype(jnp.bfloat16)

    @pl.when(upper == 0)
    def _():
        if earlier:
            out[...] = earlier[0][...]
        out[pl.ds(pl.multiple_of(here, LANES), chunk), :] = own[...]
        out[pl.ds(pl.multiple_of(there, LANES), chunk), :] = opposite

    @pl.when(upper == 1)
    def _():
        for block in range(rows // PLACE_ROWS):
            part = pl.ds(block * PLACE_ROWS, PLACE_ROWS)
            pick = pick_rows(partner, block, PLACE_ROWS, here, chunk)
            found = jnp.dot(pick, own[...], preferred_element_type=jnp.float32)
            pick = pick_rows(partner, block, PLACE_ROWS, there, chunk)
            found += jnp.dot(pick, opposite, preferred_element_type=jnp.float32)
            if earlier:
                found += earlier[0][part, :].astype(jnp.float32)
            out[part, :] = found.astype(jnp.bfloat16)


def place_own_kernel(begin, partner, own, earlier, out, picks):
    rows, chunk = out.shape[0], own.shape[0]
    upper = upper_side()
    here = upper * (rows // 2) + begin
    there = (1 - upper) * (rows // 2) + begin

    @pl.when(upper == 0)
    def _():
        out[...] = earlier[...]
        out[pl.ds(pl.multiple_of(here, LANES), chunk), :] = own[...]

    @pl.when(upper == 1)
    def _():
        for block in range(rows // PLACE_ROWS):
            part = pl.ds(block * PLACE_ROWS, PLACE_ROWS)
            pick = pick_rows(partner, block, PLACE_ROWS, here, chunk)
            found = jnp.dot(pick, own[...], preferred_element_type=jnp.float32)
            out[part, :] = (found + earlier[part, :].astype(jnp.float32)).astype(jnp.bfloat16)
            picks[part, :] = pick_rows(partner, block, PLACE_ROWS, there, chunk)


def place_other_kernel(begin, earlier, picks, other, out, held, arrivals):
    rows, chunk = held.shape[0], other.shape[0]
    upper = upper_side()
    there = (1 - upper) * (rows // 2) + begin
    size = chunk // 2

    def leave(block):
        part = pl.ds(block * size, size)
        return pltpu.make_async_copy(held.at[part, :], out.at[part, :], arrivals.at[block])

    opposite = exchanged(other[...].astype(jnp.float32)).astype(jnp.bfloat16)

    @pl.when(upper == 0)
    def _():
        for block in range(rows // size):
            part = pl.ds(block * size, size)
            half = opposite[size * (block % 2) : size * (block % 2 + 1), :]
            held[part, :] = jnp.where(there == block // 2 * chunk, half, earlier[part, :])
            leave(block).start()

    @pl.when(upper == 1)
    def _():
        for block in range(rows // size):
            part = pl.ds(block * size, size)
            found = jnp.dot(picks[part, :], opposite, preferred_element_type=jnp.float32)
            held[part, :] = (found + earlier[part, :].astype(jnp.float32)).astype(jnp.bfloat16)
            leave(block).start()

    for block in range(rows // size):
        leave(block).wait()


def split_index(values, count):
    high = jnp.floor((values.astype(jnp.float32) + 0.5) * (1.0 / count)).astype(jnp.int32)
    return high, values - high * count


def lookup(table, positions):
    found = jnp.zeros(positions.shape, jnp.float32)
    for begin in range(0, table.shape[1], LANES):
        size = min(LANES, table.shape[1] - begin)
        part = jnp.broadcast_to(table[:, begin : begin + size], (size, size))
        down = lax.broadcasted_iota(jnp.int32, (size, size), 0)
        across = lax.broadcasted_iota(jnp.int32, (size, size), 1)
        column = jnp.sum(jnp.where(down == across, part, 0.0), axis=1, keepdims=True)
        entry = begin + lax.broadcasted_iota(jnp.int32, (size, positions.shape[1]), 0)
        found += jnp.sum(jnp.where(entry == positions, column, 0.0), axis=0, keepdims=True)
    return found


def energy_kernel(pair_index, occ_energy, vir_energy, occ_lower, occ_upper, vir_sum):
    half = occ_lower.shape[1]
    for out, begin in ((occ_lower, 0), (occ_upper, half)):
        first, second = split_index(pair_index[:, pl.ds(begin, half)], NOCC)
        out[...] = lookup(occ_energy[...], first) + lookup(occ_energy[...], second)
    width = vir_sum.shape[1]
    unordered = lax.axis_index("col") * (width // 2) + lax.broadcasted_iota(jnp.int32, (1, width), 1) // 2
    first, second = split_index(unordered, NV)
    vir_sum[...] = lookup(vir_energy[...], first) + lookup(vir_energy[...], second)


def across_rows(value):
    count = lax.axis_size("row")
    return lax.ppermute(value, "row", [(i, i ^ (count // 2)) for i in range(count)])


def across_pair(value):
    return lax.ppermute(value, "col", [(i, i ^ 1) for i in range(lax.axis_size("col"))])


def two_along(value):
    count = lax.axis_size("col")
    return lax.ppermute(value, "col", [(i, (i + 2) % count) for i in range(count)])


def shards(amplitudes, integrals, pair_index, partner, occ_energy, vir_energy):
    rows, width = amplitudes.shape
    half = rows // 2
    chunks = [half * share // sum(SHARES) for share in SHARES]
    begins = [sum(chunks[:index]) for index in range(len(chunks))]
    whole_shape = jax.ShapeDtypeStruct((rows, width), jnp.bfloat16)

    def chunk_shape(index):
        return jax.ShapeDtypeStruct((chunks[index], width), jnp.bfloat16)

    def coded_shape(index):
        return jax.ShapeDtypeStruct((chunks[index] * (width // LANES) + SCALE_ROWS, LANES), jnp.int16)

    half_shape = jax.ShapeDtypeStruct((1, half), jnp.float32)
    energy_shapes = [half_shape, half_shape, jax.ShapeDtypeStruct((1, width), jnp.float32)]

    own, other, moved, crossed, arrived, done, placed = {}, {}, {}, {}, {}, {}, ()
    operands = [pltpu.with_memory_space_constraint(value, pltpu.HBM) for value in (partner[None, :], amplitudes)]
    room = (pltpu.VMEM((1, rows), jnp.int32), pltpu.SemaphoreType.DMA((rows // chunks[0] + 1,)))
    result, held = call(align_first_kernel, [chunk_shape(0), whole_shape], operands, in_spec=HBM, scratch=room)
    other[0] = across_rows(result)
    last = (result,)
    for step, index in ORDER:
        if step == "align":
            wanted = tuple((begins[chunk], send) for chunk, send in ALIGNED[index])
            shapes = [chunk_shape(chunk) for chunk, _ in ALIGNED[index]]
            result = call(functools.partial(align_kernel, wanted), shapes, (partner[None, :], held), last)
            for (chunk, send), picked in zip(ALIGNED[index], result):
                if send:
                    other[chunk] = across_rows(picked)
                else:
                    own[chunk] = picked
            last = result[:1]
            continue
        if step == "factor":
            shapes = [jax.ShapeDtypeStruct((2 * width, width), jnp.bfloat16)] * 4
            factors = call(factor_kernel, shapes, (integrals,), last)
            last = factors[:1]
            continue
        if step == "energy":
            occ_lower, occ_upper, vir_sum = call(
                energy_kernel,
                energy_shapes,
                (pair_index[None, :], occ_energy[None, :], vir_energy[None, :]),
                last,
            )
            occ_there = across_rows(occ_upper)
            last = (vir_sum,)
            continue
        inputs = (own[index], other[index])
        if step == "first":
            result = call(first_kernel, coded_shape(index), (*inputs, factors[3]), last)
            moved[index] = two_along(result)
        elif step == "second":
            result = call(second_kernel, coded_shape(index), (*inputs, factors[1], moved[index]), last)
            crossed[index] = across_pair(result)
        elif step == "third":
            result = call(third_kernel, coded_shape(index), (*inputs, factors[2], crossed[index]), last)
            arrived[index] = two_along(result)
        elif step == "last":
            sums = (crossed[index], arrived[index], occ_lower, occ_there, vir_sum)
            result = call(functools.partial(last_kernel, begins[index]), chunk_shape(index), (*inputs, factors[0], *sums), last)
            done[index] = (result, across_rows(result))
        else:
            ready = (partner[None, :], *done[index], *placed)
            result = call(functools.partial(place_kernel, begins[index]), whole_shape, ready, last)
            placed = (result,)
        last = (result,)

    index = len(SHARES) - 1
    mine, theirs = done[index]
    picks_shape = jax.ShapeDtypeStruct((rows, chunks[index]), jnp.bfloat16)
    kernel = functools.partial(place_own_kernel, begins[index])
    most, picks = call(kernel, [whole_shape, picks_shape], (partner[None, :], mine, *placed), last)
    room = pltpu.VMEM((rows, width), jnp.bfloat16)
    arrivals = pltpu.SemaphoreType.DMA((2 * rows // chunks[index],))
    kernel = functools.partial(place_other_kernel, begins[index])
    return call(kernel, whole_shape, (most, picks, theirs), out_spec=ANY, scratch=(room, arrivals))


def solution(mesh):
    in_specs = (P("row", "col"), P("col", None), P("row"), P("row"), P(), P())
    out_specs = P("row", "col")
    return jax.shard_map(shards, mesh=mesh, in_specs=in_specs, out_specs=out_specs, check_vma=False)
```
